256 devices in a mesh: kc: 8 (over x, y_lo), kb: 16 (over z, core), occ: 2 (over y_hi).
Axes of the slice: x: 4, y: 4 (y_hi: 2, y_lo: 2; y = y_hi * 2 + y_lo), z: 8, core: 2. Of those that a mesh axis runs over, the one named last changes fastest.
Arguments:
- amplitudes: bfloat16 [16, 2, 64, 1024], P('kb'), may hold values from -6 to 6
- integrals: bfloat16 [16, 2, 32, 8, 1024], P('kb', None, None, 'occ'), may hold values from -0.109375 to 0.109375
- eps_occ: float32 [8], replicated, as said below
- eps_vir: float32 [16, 32], replicated, as said below
- conserve: int32 [16, 16], replicated, may hold values from 0 to 15, as said below
- partner: int32 [16], replicated, may hold values from 0 to 15, as said below
Outputs:
- lambda_source: float32 [16, 2, 64, 1024], P('kb', None, ('kc', 'occ'))
The draws below stay inside these ranges and needn't reach their ends.
Inputs may be any that keep to these rules, and one draw needn't show every extreme that they name: conserve[kb, kc] is the label of ka + kb - kc on the periodic 4 x 4 k-mesh for one fixed ka; for every kc it is a permutation over kb, and for every kb a permutation over kc. partner[k] is the label of -k on the same k-mesh; partner of partner is k itself. `eps_occ`: every occupied energy is a whole multiple of 1/32 from -1 to 1. `eps_vir`: every virtual energy is a whole multiple of 1/32 from -1 to 2.
All inputs are finite; a program needn't handle non-finite values.
Results may differ from the reference program's by a relative error of at most 0.0031.
Values may be sent and summed in bfloat16 or wider, within the bound.
A program may use at most 256 MiB of HBM per device.

```python
import jax
import jax.numpy as jnp
from jax import lax

KX = 4
KY = 4
NK = 16
O = 8
V = 32
KCW = 8


def kpoint_tables(key):
    layout = jax.random.permutation(jax.random.fold_in(key, 11), NK).astype(jnp.int32)
    column = jax.random.randint(jax.random.fold_in(key, 13), (), 0, KY).astype(jnp.int32)
    chosen_point = KY + column
    negated_point = (KX - 1) % KX * KY + (KY - column) % KY
    target_label = (layout[chosen_point] + NK // 2) % NK
    holder = jnp.argmax(layout == target_label).astype(jnp.int32)
    layout = layout.at[holder].set(layout[negated_point])
    layout = layout.at[negated_point].set(target_label)
    inverse = jnp.zeros((NK,), jnp.int32).at[layout].set(jnp.arange(NK, dtype=jnp.int32))
    first = inverse // KY
    second = inverse % KY
    fixed_ka = jax.random.randint(jax.random.fold_in(key, 12), (), 0, NK).astype(jnp.int32)
    along_x = (first[fixed_ka] + first[:, None] - first[None, :]) % KX
    along_y = (second[fixed_ka] + second[:, None] - second[None, :]) % KY
    conserve = layout[along_x * KY + along_y]
    negated = layout[-first % KX * KY + -second % KY]
    return (conserve.astype(jnp.int32), negated.astype(jnp.int32))


def draw_conserve(key, part):
    return kpoint_tables(key)[0]


def draw_partner(key, part):
    return kpoint_tables(key)[1]


def draw_eps_occ(key, part):
    key = jax.random.fold_in(key, 21)
    steps_drawn = jax.random.randint(key, (O,), -32, 33)
    return steps_drawn.astype(jnp.float32) / 32.0


def draw_eps_vir(key, part):
    key = jax.random.fold_in(key, 22)
    steps_drawn = jax.random.randint(key, (NK, V), -32, 65)
    return steps_drawn.astype(jnp.float32) / 32.0


def block_levels(own_key, shape, split, smallest, largest):
    def one(dim, blocks):
        steps = jax.random.uniform(jax.random.fold_in(jax.random.fold_in(own_key, 6), dim), (blocks,), jnp.float32, smallest / len(split), largest / len(split))
        return jnp.repeat(jnp.exp(steps), shape[dim] // blocks).reshape((-1,) + (1,) * (len(shape) - dim - 1))

    gain = one(*split[0])
    for cut in split[1:]:
        gain = gain * one(*cut)
    return gain


def noise(stream_key, dims, width, reach, shards=(), kind=jnp.bfloat16):
    factor_of = block_levels(stream_key, dims, shards, -0.22, 0.18) if shards else 1.0
    drawn = jax.random.normal(stream_key, dims, jnp.float32) * width * factor_of
    return jnp.minimum(jnp.maximum(drawn, -reach), reach).astype(kind)


def setup_inputs(seed: int = 0) -> dict:
    arg_keys = jax.random.split(jax.random.key(seed), 7)
    return {
        "amplitudes": noise(arg_keys[0], (NK, 2, O * O, V * V), 1.0, 6.0, ((0, 16),)),
        "integrals": noise(arg_keys[1], (NK, 2, V, O, V * V), (12 * O * V) ** -0.5, 0.109375, ((0, 16), (3, 2))),
        "eps_occ": draw_eps_occ(jax.random.fold_in(arg_keys[6], 71), 0),
        "eps_vir": draw_eps_vir(jax.random.fold_in(arg_keys[6], 71), 0),
        "conserve": draw_conserve(jax.random.fold_in(arg_keys[6], 71), 0),
        "partner": draw_partner(jax.random.fold_in(arg_keys[6], 71), 0),
    }


def full_dot(left, right):
    return jnp.dot(left, right, precision=lax.Precision.HIGHEST, preferred_element_type=jnp.float32)


def floor_signed(denominator):
    return jnp.where(denominator > 0.0, jnp.maximum(denominator, 1.0), jnp.minimum(denominator, -1.0))


def triplet_term(sym_mat, slab, row_den, col_den):
    sym_real = sym_mat[0].astype(jnp.float32)
    sym_imag = sym_mat[1].astype(jnp.float32)
    slab_real = slab[0].astype(jnp.float32)
    slab_imag = slab[1].astype(jnp.float32)
    row_count = sym_real.shape[0]
    block_rows = min(512, row_count)
    block_count = row_count // block_rows

    def one_block(inputs):
        part_real, part_imag, den_rows = inputs
        prod_real = full_dot(part_real, slab_real) - full_dot(part_imag, slab_imag)
        prod_imag = full_dot(part_real, slab_imag) + full_dot(part_imag, slab_real)
        floored = floor_signed(den_rows[:, None] + col_den[None, :])
        scaled_real = (prod_real / floored).astype(jnp.bfloat16)
        scaled_imag = (prod_imag / floored).astype(jnp.bfloat16)
        scaled_real, scaled_imag = lax.optimization_barrier((scaled_real, scaled_imag))
        scaled_real = scaled_real.astype(jnp.float32)
        scaled_imag = scaled_imag.astype(jnp.float32)
        back_real = full_dot(scaled_real, slab_real.T) + full_dot(scaled_imag, slab_imag.T)
        back_imag = full_dot(scaled_imag, slab_real.T) - full_dot(scaled_real, slab_imag.T)
        return jnp.stack([back_real, back_imag])

    blocks = lax.map(one_block, (sym_real.reshape(block_count, block_rows, -1),
                                 sym_imag.reshape(block_count, block_rows, -1),
                                 row_den.reshape(block_count, block_rows)))
    return jnp.transpose(blocks, (1, 0, 2, 3)).reshape(2, row_count, -1)


def reference(amplitudes, integrals, eps_occ, eps_vir, conserve, partner):
    pair_occ = (eps_occ[:, None] + eps_occ[None, :]).reshape(-1)

    def one_kb(kb_label):
        own_block = amplitudes[kb_label].astype(jnp.float32)
        mirror = amplitudes[partner[kb_label]].astype(jnp.float32)
        mirror = jnp.swapaxes(mirror.reshape(2, O, O, V * V), 1, 2).reshape(2, O * O, V * V)
        symmetric = jnp.stack([own_block[0] + mirror[0], own_block[1] - mirror[1]]).astype(jnp.bfloat16)
        sym_mat = symmetric.reshape(2, O * O * V, V)
        row_den = (pair_occ[:, None] - eps_vir[kb_label][None, :]).reshape(-1)

        def one_kc(running, kc_label):
            slab_label = conserve[kb_label, kc_label]
            slab = integrals[slab_label].reshape(2, V, O * V * V)
            col_den = (eps_occ[:, None, None] - eps_vir[kc_label][None, :, None]
                       - eps_vir[slab_label][None, None, :]).reshape(-1)
            return running + triplet_term(sym_mat, slab, row_den, col_den), None

        start_sum = jnp.zeros((2, O * O * V, V), jnp.float32)
        summed, _ = lax.scan(one_kc, start_sum, jnp.arange(KCW, dtype=jnp.int32))
        return summed.reshape(2, O * O, V * V)

    return lax.map(one_kb, jnp.arange(NK, dtype=jnp.int32))
```

```python
import functools

import jax
import jax.numpy as jnp
from jax import lax
from jax.experimental import pallas as pl
from jax.experimental.pallas import tpu as pltpu
from jax.sharding import PartitionSpec as P

KC = 8
KB = 16
OCC = 2
POS = KC * OCC
LANES = 128
PAIRS = 64
GROUPS = 8
HALF = 32
ROWS = GROUPS * HALF
DEPTH = 32
TILES = 32
CHUNK = 16
SHIFT = 2.0**-18
MESH = pl.DeviceIdType.MESH
F32 = jnp.float32
BF16 = jnp.bfloat16


def place(position, kb):
    return {"kc": position // OCC, "kb": kb, "occ": position % OCC}


def kernel(
    conserve, partner, eps_occ, eps_vir, amp, slab, out,
    abuf, symbuf, lhs, ztop, zbot, row_den, col_den, acc, o1_send, o1_recv0, o1_recv1, o2_send, o2_recv,
    beta, holder, copy_sem, h1_send, h1_recv, h2_send, h2_recv, p1_send, p1_recv, p2_send, p2_recv,
):
    kc = lax.axis_index("kc")
    kb = lax.axis_index("kb")
    occ = lax.axis_index("occ")
    pos = kc * OCC + occ
    core = kb % 2
    plane = kb - core
    spot = pos * 2 + core
    part = pos // GROUPS
    group = pos % GROUPS

    o1_recv = (o1_recv0, o1_recv1)
    barrier = pltpu.get_barrier_semaphore()

    @pl.loop(1, KB)
    def _(step):
        pl.semaphore_signal(
            barrier, inc=1, device_id=place(pos, (kb + step) % KB), device_id_type=MESH
        )

    @pl.loop(1, POS)
    def _(step):
        for other in range(2):
            pl.semaphore_signal(
                barrier,
                inc=1,
                device_id=place((pos + step) % POS, plane + other),
                device_id_type=MESH,
            )

    own = pltpu.make_async_copy(
        amp.at[0, part, :, pl.ds(pl.multiple_of(group * LANES, LANES), LANES)],
        abuf.at[kb],
        copy_sem,
    )
    own.start()
    own.wait()
    pl.semaphore_wait(barrier, KB - 1 + 2 * (POS - 1))

    @pl.loop(1, KB)
    def _(step):
        pltpu.make_async_remote_copy(
            src_ref=abuf.at[kb],
            dst_ref=abuf.at[kb],
            send_sem=h1_send,
            recv_sem=h1_recv,
            device_id=place(pos, (kb + step) % KB),
            device_id_type=MESH,
        ).start()

    ztop[...] = jnp.zeros_like(ztop)
    zbot[...] = jnp.zeros_like(zbot)
    for k in range(4):
        real = slab[0, 0, :, k, :]
        imag = slab[0, 1, :, k, :]
        for u in range(8):
            at = (k * 8 + u) * 2 * LANES
            re = real[:, u * LANES : (u + 1) * LANES]
            im = imag[:, u * LANES : (u + 1) * LANES]
            ztop[3 * DEPTH : 4 * DEPTH, at : at + LANES] = re
            ztop[3 * DEPTH : 4 * DEPTH, at + LANES : at + 2 * LANES] = im
            zbot[3 * DEPTH : 4 * DEPTH, at : at + LANES] = -im
            zbot[3 * DEPTH : 4 * DEPTH, at + LANES : at + 2 * LANES] = re

    for p in range(KC):
        found = jnp.int32(0)
        for label in range(KB):
            found = found + jnp.where(conserve[label, p] == kb, label, 0)
        beta[p] = jnp.minimum(found, KB - 1)
    for c in range(2):
        for label in range(KB):
            left = jnp.int32(KC)
            for p in range(KC):
                left = left - jnp.where(conserve[label, p] == plane + c, KC - p, 0)
            holder[c * KB + label] = jnp.maximum(left, 0)
    mine = jnp.int32(0)
    for label in range(KB):
        mine = mine + jnp.where(conserve[label, kc] == kb, label, 0)
    mine = jnp.minimum(mine, KB - 1)

    row = lax.broadcasted_iota(jnp.int32, (HALF, LANES), 0)
    lane = lax.broadcasted_iota(jnp.int32, (8, LANES), 1)
    for h in range(2):
        i_of = row // 4
        j_of = (row // 2) % 2 * 4 + h * 2 + row % 2
        pair = jnp.full((HALF, LANES), -SHIFT, F32)
        for k in range(8):
            pair = pair + jnp.where(i_of == k, eps_occ[k], 0.0)
            pair = pair + jnp.where(j_of == k, eps_occ[k], 0.0)
        for a in range(DEPTH):
            g, sub = a // 4, a % 4
            row_den[h, sub, g * HALF : (g + 1) * HALF, :] = pair - eps_vir[mine, a]
    vir_c = jnp.zeros((8, LANES), F32)
    for c in range(DEPTH):
        vir_c = vir_c + jnp.where(lane % DEPTH == c, eps_vir[kb, c], 0.0)
    for u in range(8):
        vir_bc = vir_c
        for s in range(4):
            vir_bc = vir_bc + jnp.where(lane // DEPTH == s, eps_vir[kc, u * 4 + s], 0.0)
        for k in range(4):
            col_den[k * 8 + u] = eps_occ[occ * 4 + k] - vir_bc

    for zero in range(4):
        o1_recv0[2 * POS + zero] = jnp.zeros((16, LANES), BF16)
        o1_recv1[2 * POS + zero] = jnp.zeros((16, LANES), BF16)

    out_row = lax.broadcasted_iota(jnp.int32, (PAIRS, 2 * PAIRS), 0)
    in_col = lax.broadcasted_iota(jnp.int32, (PAIRS, 2 * PAIRS), 1)
    h_of = out_row // HALF
    i_of = out_row % HALF // 4
    j_of = out_row % HALF // 2 % 2 * 4 + h_of * 2 + out_row % 2
    sign = (1 - 2 * part).astype(F32)
    order = jnp.where(in_col == i_of * 8 + j_of, 1.0, 0.0) + jnp.where(
        in_col == PAIRS + j_of * 8 + i_of, sign, 0.0
    )
    order = order.astype(BF16)

    whole = pltpu.make_async_remote_copy(
        src_ref=abuf.at[pl.ds(0, KB - 1)],
        dst_ref=abuf.at[pl.ds(0, KB - 1)],
        send_sem=h1_send,
        recv_sem=h1_recv,
        device_id=place(pos, (kb + 1) % KB),
        device_id_type=MESH,
    )
    whole.wait_recv()
    for p in range(KC):
        label = beta[p]
        both = jnp.concatenate([abuf[label], abuf[partner[label]]], axis=0)
        sym = jnp.dot(order, both, preferred_element_type=F32).astype(BF16)
        symbuf[0, p] = sym[:HALF]
        symbuf[1, p] = sym[HALF:]
    for h in range(2):
        lhs[h, pos] = symbuf[h, kc]

        @pl.loop(1, POS)
        def _(step):
            to = (pos + step) % POS
            pltpu.make_async_remote_copy(
                src_ref=symbuf.at[h, to // OCC],
                dst_ref=lhs.at[h, pos],
                send_sem=h2_send.at[h],
                recv_sem=h2_recv.at[h],
                device_id=place(to, kb),
                device_id_type=MESH,
            ).start()

    perm_row = lax.broadcasted_iota(jnp.int32, (ROWS, ROWS), 0)
    perm_col = lax.broadcasted_iota(jnp.int32, (ROWS, ROWS), 1)
    perm_from = perm_row % 16 // 2 * HALF + perm_row // 16 * 2 + perm_row % 2
    perm = jnp.where(perm_col == perm_from, 1.0, 0.0).astype(BF16)

    def lhs_wait(h):
        return pltpu.make_async_remote_copy(
            src_ref=lhs.at[h, pl.ds(0, POS - 1)],
            dst_ref=lhs.at[h, pl.ds(0, POS - 1)],
            send_sem=h2_send.at[h],
            recv_sem=h2_recv.at[h],
            device_id=place((pos + 1) % POS, kb),
            device_id_type=MESH,
        )

    def multiply(h, first, last):
        left = jnp.concatenate(
            [
                lhs[h, 0:GROUPS].reshape(ROWS, LANES),
                lhs[h, GROUPS:POS].reshape(ROWS, LANES),
            ],
            axis=1,
        )

        @pl.loop(first, last)
        def _(step):
            sub = step // (TILES // CHUNK)
            chunk = step % (TILES // CHUNK)
            at = pl.multiple_of(chunk * (CHUNK * 2 * LANES), CHUNK * 2 * LANES)
            down = pl.multiple_of((3 - sub) * DEPTH, DEPTH)
            weight = jnp.concatenate(
                [
                    ztop[pl.ds(down, 4 * DEPTH), pl.ds(at, CHUNK * 2 * LANES)],
                    zbot[pl.ds(down, 4 * DEPTH), pl.ds(at, CHUNK * 2 * LANES)],
                ],
                axis=0,
            )
            product = jnp.dot(left, weight, preferred_element_type=F32)
            den_row = row_den[h, sub]
            parts = []
            for s in range(CHUNK):
                den = den_row + col_den[chunk * CHUNK + s, 0:1, :]
                inverse = jnp.clip(pltpu.reciprocal(den, approx=True), -1.0, 1.0)
                lo = s * 2 * LANES
                parts.append((product[:, lo : lo + LANES] * inverse).astype(BF16))
                parts.append((product[:, lo + LANES : lo + 2 * LANES] * inverse).astype(BF16))
            scaled = jnp.concatenate(parts, axis=1)
            acc[...] += lax.dot_general(
                scaled, weight, (((1,), (1,)), ((), ())), preferred_element_type=F32
            )

    def send_partials(h):
        packed = jnp.dot(perm, acc[...].astype(BF16), preferred_element_type=F32).astype(BF16)
        for r in range(POS):
            for c in range(2):
                o1_send[h, r * 2 + c] = packed[r * 16 : (r + 1) * 16, c * LANES : (c + 1) * LANES]
        o1_recv[h][spot] = o1_send[h, spot]

        @pl.loop(1, 2 * POS)
        def _(step):
            to = (spot + step) % (2 * POS)
            pltpu.make_async_remote_copy(
                src_ref=o1_send.at[h, to],
                dst_ref=o1_recv[h].at[spot],
                send_sem=p1_send.at[h],
                recv_sem=p1_recv.at[h],
                device_id=place(to // 2, plane + to % 2),
                device_id_type=MESH,
            ).start()

    def partials_wait(h):
        return pltpu.make_async_remote_copy(
            src_ref=o1_send.at[h, pl.ds(0, 2 * POS - 1)],
            dst_ref=o1_recv[h].at[pl.ds(0, 2 * POS - 1)],
            send_sem=p1_send.at[h],
            recv_sem=p1_recv.at[h],
            device_id=place((pos + 1) % POS, kb),
            device_id_type=MESH,
        )

    def send_sums(h):
        partials_wait(h).wait_recv()

        for label in range(KB):
            total = jnp.zeros((16, LANES), F32)
            for c in range(2):
                p = holder[c * KB + label]
                for o in range(OCC):
                    total = total + o1_recv[h][(p * OCC + o) * 2 + c].astype(F32)
            o2_send[h, label] = total.astype(BF16)
        o2_recv[h, kb] = o2_send[h, kb]

        @pl.loop(1, KB)
        def _(step):
            to = (kb + step) % KB
            pltpu.make_async_remote_copy(
                src_ref=o2_send.at[h, to],
                dst_ref=o2_recv.at[h, kb],
                send_sem=p2_send.at[h],
                recv_sem=p2_recv.at[h],
                device_id=place(pos, to),
                device_id_type=MESH,
            ).start()

    def sums_wait(h):
        return pltpu.make_async_remote_copy(
            src_ref=o2_send.at[h, pl.ds(0, KB - 1)],
            dst_ref=o2_recv.at[h, pl.ds(0, KB - 1)],
            send_sem=p2_send.at[h],
            recv_sem=p2_recv.at[h],
            device_id=place(pos, (kb + 1) % KB),
            device_id_type=MESH,
        )

    def finish(h):
        sums_wait(h).wait_recv()
        for c in range(2):
            total = jnp.zeros((16, LANES), F32)
            for z in range(KB // 2):
                total = total + o2_recv[h, z * 2 + c].astype(F32)
            out[h, c] = total

    steps = 4 * TILES // CHUNK
    lhs_wait(0).wait_recv()
    acc[...] = jnp.zeros_like(acc)
    multiply(0, 0, steps)
    send_partials(0)
    lhs_wait(1).wait_recv()
    acc[...] = jnp.zeros_like(acc)
    multiply(1, 0, steps // 2)
    send_sums(0)
    multiply(1, steps // 2, steps)
    send_partials(1)
    finish(0)
    send_sums(1)
    whole.wait_send()
    for h in range(2):
        lhs_wait(h).wait_send()
        partials_wait(h).wait_send()
    finish(1)
    for h in range(2):
        sums_wait(h).wait_send()


def shards(amplitudes, integrals, eps_occ, eps_vir, conserve, partner):
    smem = pl.BlockSpec(memory_space=pltpu.SMEM)
    vmem = pl.BlockSpec(memory_space=pltpu.VMEM)
    result = pl.pallas_call(
        kernel,
        out_shape=jax.ShapeDtypeStruct((2, 2, 16, LANES), F32),
        in_specs=[smem, smem, smem, smem, pl.BlockSpec(memory_space=pl.ANY), vmem],
        out_specs=vmem,
        scratch_shapes=[
            pltpu.VMEM((KB, PAIRS, LANES), BF16),
            pltpu.VMEM((2, KC, HALF, LANES), BF16),
            pltpu.VMEM((2, POS, HALF, LANES), BF16),
            pltpu.VMEM((7 * DEPTH, TILES * 2 * LANES), BF16),
            pltpu.VMEM((7 * DEPTH, TILES * 2 * LANES), BF16),
            pltpu.VMEM((2, 4, ROWS, LANES), F32),
            pltpu.VMEM((TILES, 8, LANES), F32),
            pltpu.VMEM((ROWS, 2 * LANES), F32),
            pltpu.VMEM((2, 2 * POS, 16, LANES), BF16),
            pltpu.VMEM((2 * POS + 4, 16, LANES), BF16),
            pltpu.VMEM((2 * POS + 4, 16, LANES), BF16),
            pltpu.VMEM((2, KB, 16, LANES), BF16),
            pltpu.VMEM((2, KB, 16, LANES), BF16),
            pltpu.SMEM((KC,), jnp.int32),
            pltpu.SMEM((2 * KB,), jnp.int32),
            pltpu.SemaphoreType.DMA,
            pltpu.SemaphoreType.DMA,
            pltpu.SemaphoreType.DMA,
        ]
        + [pltpu.SemaphoreType.DMA((2,))] * 6,
        compiler_params=pltpu.CompilerParams(
            collective_id=0, has_side_effects=True, vmem_limit_bytes=60 * 2**20
        ),
        name="lambda_source",
    )(conserve, partner, eps_occ, eps_vir, amplitudes, integrals)
    result = result.reshape(2, 2, GROUPS, 2, LANES)
    return jnp.transpose(result, (1, 0, 3, 2, 4)).reshape(1, 2, 4, GROUPS * LANES)


def solution(mesh):
    in_specs = (P("kb", None, None, None), P("kb", None, None, "occ", None), P(), P(), P(), P())
    out_specs = P("kb", None, ("kc", "occ"), None)
    return jax.shard_map(shards, mesh=mesh, in_specs=in_specs, out_specs=out_specs, check_vma=False)
```

```python
import functools

import jax
import jax.numpy as jnp
from jax import lax
from jax.experimental import pallas as pl
from jax.experimental.pallas import tpu as pltpu
from jax.sharding import PartitionSpec as P

KC = 8
KB = 16
OCC = 2
POS = KC * OCC
LANES = 128
PAIRS = 64
GROUPS = 8
HALF = 32
ROWS = GROUPS * HALF
DEPTH = 32
TILES = 32
CHUNK = 32
SHIFT = 2.0**-18
DEEP = 8
ORDER = (1, 7, 2, 6, 3, 5, 4)
MESH = pl.DeviceIdType.MESH
F32 = jnp.float32
BF16 = jnp.bfloat16


def place(position, kb):
    return {"kc": position // OCC, "kb": kb, "occ": position % OCC}


def kernel(
    conserve_in, partner_in, eps_occ_in, eps_vir_in, amp, slab_in, out,
    conserve, partner, eps_occ, eps_vir, slab, load_sem, abuf, symbuf, lhs, ztop, zbot, row_den, col_den, acc, o1_send, o1_recv0, o1_recv1,
    sums, sums_recv, o2_send, o2_recv, last_send, last_recv, beta, holder, ready, copy_sem, h1_send, h1_recv, fwd_send, fwd_recv,
    h2_send, h2_recv, p1_send, p1_recv, sib_send, sib_recv, p2_send, p2_recv, last_sems,
):
    kc = lax.axis_index("kc")
    kb = lax.axis_index("kb")
    occ = lax.axis_index("occ")
    pos = kc * OCC + occ
    core = kb % 2
    z = kb // 2
    sibling = {"kb": kb + 1 - 2 * core}
    part = pos // GROUPS
    group = pos % GROUPS
    x = kc // 2
    y_lo = kc % 2
    y = occ * 2 + y_lo

    def along_z(step):
        return {"kb": (z + step) % DEEP * 2 + core}

    def along_y(step):
        to = (y + step) % 4
        return {"kc": x * 2 + to % 2, "occ": to // 2}

    o1_recv = (o1_recv0, o1_recv1)
    barrier = pltpu.get_barrier_semaphore()

    for step in ORDER:
        pl.semaphore_signal(barrier, inc=1, device_id=along_z(step), device_id_type=MESH)
    pl.semaphore_signal(barrier, inc=1, device_id=sibling, device_id_type=MESH)
    for step in range(1, 4):
        pl.semaphore_signal(
            barrier,
            inc=1,
            device_id={"kc": (x + step) % 4 * 2 + y_lo},
            device_id_type=MESH,
        )
        pl.semaphore_signal(barrier, inc=1, device_id=along_y(step), device_id_type=MESH)

    own = pltpu.make_async_copy(
        amp.at[0, part, :, pl.ds(pl.multiple_of(group * LANES, LANES), LANES)],
        abuf.at[kb],
        copy_sem,
    )
    own.start()
    loads = [
        pltpu.make_async_copy(source, target, load_sem.at[at])
        for at, (source, target) in enumerate(
            (
                (slab_in, slab),
                (conserve_in, conserve),
                (partner_in, partner),
                (eps_occ_in, eps_occ),
                (eps_vir_in, eps_vir),
            )
        )
    ]
    for load in loads:
        load.start()
    own.wait()
    pl.semaphore_wait(barrier, DEEP + 6)

    def stripe_copy(step):
        return pltpu.make_async_remote_copy(
            src_ref=abuf.at[kb],
            dst_ref=abuf.at[kb],
            send_sem=h1_send,
            recv_sem=h1_recv.at[z],
            device_id=along_z(step),
            device_id_type=MESH,
        )

    def forward(label):
        pltpu.make_async_remote_copy(
            src_ref=abuf.at[label],
            dst_ref=abuf.at[label],
            send_sem=fwd_send,
            recv_sem=fwd_recv,
            device_id=sibling,
            device_id_type=MESH,
        ).start()

    for step in ORDER:
        stripe_copy(step).start()
    for step in range(1, 4):
        pl.semaphore_signal(ready, inc=1, device_id=along_y(step), device_id_type=MESH)
    forward(kb)

    ztop[...] = jnp.zeros_like(ztop)
    zbot[...] = jnp.zeros_like(zbot)
    for load in loads:
        load.wait()
    for k in range(4):
        real = slab[0, 0, :, k, :]
        imag = slab[0, 1, :, k, :]
        for u in range(8):
            at = (k * 8 + u) * 2 * LANES
            re = real[:, u * LANES : (u + 1) * LANES]
            im = imag[:, u * LANES : (u + 1) * LANES]
            ztop[3 * DEPTH : 4 * DEPTH, at : at + LANES] = re
            ztop[3 * DEPTH : 4 * DEPTH, at + LANES : at + 2 * LANES] = im
            zbot[3 * DEPTH : 4 * DEPTH, at : at + LANES] = -im
            zbot[3 * DEPTH : 4 * DEPTH, at + LANES : at + 2 * LANES] = re

    for p in range(KC):
        found = jnp.int32(0)
        for label in range(KB):
            found = found + jnp.where(conserve[label, p] == kb, label, 0)
        beta[p] = jnp.minimum(found, KB - 1)
    for label in range(KB):
        left = jnp.int32(KC)
        for p in range(KC):
            left = left - jnp.where(conserve[label, p] == kb, KC - p, 0)
        holder[label] = jnp.maximum(left, 0)
    mine = jnp.int32(0)
    for label in range(KB):
        mine = mine + jnp.where(conserve[label, kc] == kb, label, 0)
    mine = jnp.minimum(mine, KB - 1)

    row = lax.broadcasted_iota(jnp.int32, (HALF, LANES), 0)
    lane = lax.broadcasted_iota(jnp.int32, (8, LANES), 1)
    for h in range(2):
        i_of = row // 4
        j_of = (row // 2) % 2 * 4 + h * 2 + row % 2
        pair = jnp.full((HALF, LANES), -SHIFT, F32)
        for k in range(8):
            pair = pair + jnp.where(i_of == k, eps_occ[k], 0.0)
            pair = pair + jnp.where(j_of == k, eps_occ[k], 0.0)
        for a in range(DEPTH):
            g, sub = a // 4, a % 4
            row_den[h, sub, g * HALF : (g + 1) * HALF, :] = pair - eps_vir[mine, a]
    vir_c = jnp.zeros((8, LANES), F32)
    for c in range(DEPTH):
        vir_c = vir_c + jnp.where(lane % DEPTH == c, eps_vir[kb, c], 0.0)
    for u in range(8):
        vir_bc = vir_c
        for s in range(4):
            vir_bc = vir_bc + jnp.where(lane // DEPTH == s, eps_vir[kc, u * 4 + s], 0.0)
        for k in range(4):
            col_den[k * 8 + u] = eps_occ[occ * 4 + k] - vir_bc

    for zero in range(OCC):
        o1_recv0[POS + zero] = jnp.zeros((16, 2 * LANES), BF16)
        o1_recv1[POS + zero] = jnp.zeros((16, 2 * LANES), BF16)

    out_row = lax.broadcasted_iota(jnp.int32, (PAIRS, 2 * PAIRS), 0)
    in_col = lax.broadcasted_iota(jnp.int32, (PAIRS, 2 * PAIRS), 1)
    h_of = out_row // HALF
    i_of = out_row % HALF // 4
    j_of = out_row % HALF // 2 % 2 * 4 + h_of * 2 + out_row % 2
    sign = (1 - 2 * part).astype(F32)
    order = jnp.where(in_col == i_of * 8 + j_of, 1.0, 0.0) + jnp.where(
        in_col == PAIRS + j_of * 8 + i_of, sign, 0.0
    )
    order = order.astype(BF16)

    perm_row = lax.broadcasted_iota(jnp.int32, (ROWS, ROWS), 0)
    perm_col = lax.broadcasted_iota(jnp.int32, (ROWS, ROWS), 1)
    perm_from = perm_row % 16 // 2 * HALF + perm_row // 16 * 2 + perm_row % 2
    perm = jnp.where(perm_col == perm_from, 1.0, 0.0).astype(BF16)

    for step in ORDER:
        came = (z + DEEP - step) % DEEP
        pltpu.make_async_remote_copy(
            src_ref=abuf.at[kb],
            dst_ref=abuf.at[kb],
            send_sem=h1_send,
            recv_sem=h1_recv.at[came],
            device_id=sibling,
            device_id_type=MESH,
        ).wait_recv()
        forward(came * 2 + core)
    forwarded = pltpu.make_async_remote_copy(
        src_ref=abuf.at[pl.ds(0, DEEP)],
        dst_ref=abuf.at[pl.ds(0, DEEP)],
        send_sem=fwd_send,
        recv_sem=fwd_recv,
        device_id=sibling,
        device_id_type=MESH,
    )
    forwarded.wait_recv()
    pl.semaphore_wait(ready, 3)
    for p in range(KC):
        label = beta[p]
        both = jnp.concatenate([abuf[label], abuf[partner[label]]], axis=0)
        sym = jnp.dot(order, both, preferred_element_type=F32).astype(BF16)
        symbuf[0, p] = sym[:HALF]
        symbuf[1, p] = sym[HALF:]
    def send_rows(h):
        lhs[h, pos] = symbuf[h, kc]

        @pl.loop(1, POS)
        def _(step):
            to = (pos + step) % POS
            pltpu.make_async_remote_copy(
                src_ref=symbuf.at[h, to // OCC],
                dst_ref=lhs.at[h, pos],
                send_sem=h2_send.at[h],
                recv_sem=h2_recv.at[h],
                device_id=place(to, kb),
                device_id_type=MESH,
            ).start()

    def lhs_wait(h):
        return pltpu.make_async_remote_copy(
            src_ref=lhs.at[h, pl.ds(0, POS - 1)],
            dst_ref=lhs.at[h, pl.ds(0, POS - 1)],
            send_sem=h2_send.at[h],
            recv_sem=h2_recv.at[h],
            device_id=sibling,
            device_id_type=MESH,
        )

    def multiply(h, first, last):
        left = jnp.concatenate(
            [
                lhs[h, 0:GROUPS].reshape(ROWS, LANES),
                lhs[h, GROUPS:POS].reshape(ROWS, LANES),
            ],
            axis=1,
        )

        @pl.loop(first, last)
        def _(step):
            sub = step // (TILES // CHUNK)
            chunk = step % (TILES // CHUNK)
            at = pl.multiple_of(chunk * (CHUNK * 2 * LANES), CHUNK * 2 * LANES)
            down = pl.multiple_of((3 - sub) * DEPTH, DEPTH)
            weight = jnp.concatenate(
                [
                    ztop[pl.ds(down, 4 * DEPTH), pl.ds(at, CHUNK * 2 * LANES)],
                    zbot[pl.ds(down, 4 * DEPTH), pl.ds(at, CHUNK * 2 * LANES)],
                ],
                axis=0,
            )
            product = jnp.dot(left, weight, preferred_element_type=F32)
            den_row = row_den[h, sub]
            parts = []
            for s in range(CHUNK):
                den = den_row + col_den[chunk * CHUNK + s, 0:1, :]
                inverse = jnp.clip(pltpu.reciprocal(den, approx=True), -1.0, 1.0)
                lo = s * 2 * LANES
                parts.append((product[:, lo : lo + LANES] * inverse).astype(BF16))
                parts.append((product[:, lo + LANES : lo + 2 * LANES] * inverse).astype(BF16))
            scaled = jnp.concatenate(parts, axis=1)
            acc[...] += lax.dot_general(
                scaled, weight, (((1,), (1,)), ((), ())), preferred_element_type=F32
            )

    def send_partials(h):
        packed = jnp.dot(perm, acc[...].astype(BF16), preferred_element_type=F32).astype(BF16)
        for r in range(POS):
            o1_send[h, r] = packed[r * 16 : (r + 1) * 16]
        o1_recv[h][pos] = o1_send[h, pos]

        @pl.loop(1, POS)
        def _(step):
            to = (pos + step) % POS
            pltpu.make_async_remote_copy(
                src_ref=o1_send.at[h, to],
                dst_ref=o1_recv[h].at[pos],
                send_sem=p1_send.at[h],
                recv_sem=p1_recv.at[h],
                device_id=place(to, kb),
                device_id_type=MESH,
            ).start()

    def partials_wait(h):
        return pltpu.make_async_remote_copy(
            src_ref=o1_send.at[h, pl.ds(0, POS - 1)],
            dst_ref=o1_recv[h].at[pl.ds(0, POS - 1)],
            send_sem=p1_send.at[h],
            recv_sem=p1_recv.at[h],
            device_id=sibling,
            device_id_type=MESH,
        )

    def core_copy(h):
        return pltpu.make_async_remote_copy(
            src_ref=sums.at[h, 1 - core],
            dst_ref=sums_recv.at[h],
            send_sem=sib_send.at[h],
            recv_sem=sib_recv.at[h],
            device_id=sibling,
            device_id_type=MESH,
        )

    def sum_plane(h):
        partials_wait(h).wait_recv()
        for label in range(KB):
            p = holder[label]
            total = o1_recv[h][p * OCC].astype(F32) + o1_recv[h][p * OCC + 1].astype(F32)
            sums[h, 0, label] = total[:, :LANES]
            sums[h, 1, label] = total[:, LANES:]
        core_copy(h).start()

    def send_sums(h):
        core_copy(h).wait_recv()
        o2_send[h] = (sums[h, core] + sums_recv[h]).astype(BF16)
        o2_recv[h, z] = o2_send[h, pl.ds(2 * z, 2)]
        for step in ORDER:
            pltpu.make_async_remote_copy(
                src_ref=o2_send.at[h, pl.ds((z + step) % DEEP * 2, 2)],
                dst_ref=o2_recv.at[h, z],
                send_sem=p2_send.at[h],
                recv_sem=p2_recv.at[h],
                device_id=along_z(step),
                device_id_type=MESH,
            ).start()

    def sums_wait(h):
        return pltpu.make_async_remote_copy(
            src_ref=o2_recv.at[h, pl.ds(0, DEEP - 1)],
            dst_ref=o2_recv.at[h, pl.ds(0, DEEP - 1)],
            send_sem=p2_send.at[h],
            recv_sem=p2_recv.at[h],
            device_id=sibling,
            device_id_type=MESH,
        )

    def last_copy(h):
        return pltpu.make_async_remote_copy(
            src_ref=last_send.at[h, 1 - core],
            dst_ref=last_recv.at[h],
            send_sem=last_sems.at[h],
            recv_sem=last_sems.at[2 + h],
            device_id=sibling,
            device_id_type=MESH,
        )

    def send_last(h):
        sums_wait(h).wait_recv()
        for c in range(2):
            total = o2_recv[h, 0, c].astype(F32)
            for deep in range(1, DEEP):
                total = total + o2_recv[h, deep, c].astype(F32)
            last_send[h, c] = total
        last_copy(h).start()

    def finish(h):
        last_copy(h).wait_recv()
        for at, total in ((core, last_send[h, core]), (1 - core, last_recv[h])):
            for g in range(GROUPS):
                out[0, at, 2 * h : 2 * h + 2, g * LANES : (g + 1) * LANES] = total[2 * g : 2 * g + 2]

    steps = 4 * TILES // CHUNK
    send_rows(0)
    lhs_wait(0).wait_recv()
    send_rows(1)
    acc[...] = jnp.zeros_like(acc)
    multiply(0, 0, steps)
    send_partials(0)
    lhs_wait(1).wait_recv()
    acc[...] = jnp.zeros_like(acc)
    multiply(1, 0, steps // 2)
    sum_plane(0)
    multiply(1, steps // 2, 3 * steps // 4)
    send_sums(0)
    multiply(1, 3 * steps // 4, steps)
    send_partials(1)
    send_last(0)
    sum_plane(1)
    finish(0)
    send_sums(1)
    pltpu.make_async_remote_copy(
        src_ref=abuf.at[pl.ds(0, DEEP - 1)],
        dst_ref=abuf.at[pl.ds(0, DEEP - 1)],
        send_sem=h1_send,
        recv_sem=fwd_recv,
        device_id=sibling,
        device_id_type=MESH,
    ).wait_send()
    forwarded.wait_send()
    for h in range(2):
        lhs_wait(h).wait_send()
        partials_wait(h).wait_send()
        core_copy(h).wait_send()
    send_last(1)
    finish(1)
    for h in range(2):
        sums_wait(h).wait_send()
        last_copy(h).wait_send()


def shards(amplitudes, integrals, eps_occ, eps_vir, conserve, partner):
    return pl.pallas_call(
        kernel,
        out_shape=jax.ShapeDtypeStruct((1, 2, 4, GROUPS * LANES), F32),
        in_specs=[pl.BlockSpec(memory_space=pl.ANY)] * 6,
        out_specs=pl.BlockSpec(memory_space=pltpu.VMEM),
        scratch_shapes=[
            pltpu.SMEM((KB, KB), jnp.int32),
            pltpu.SMEM((KB,), jnp.int32),
            pltpu.SMEM((8,), F32),
            pltpu.SMEM((KB, DEPTH), F32),
            pltpu.VMEM((1, 2, DEPTH, 4, 1024), BF16),
            pltpu.SemaphoreType.DMA((5,)),
            pltpu.VMEM((KB, PAIRS, LANES), BF16),
            pltpu.VMEM((2, KC, HALF, LANES), BF16),
            pltpu.VMEM((2, POS, HALF, LANES), BF16),
            pltpu.VMEM((7 * DEPTH, TILES * 2 * LANES), BF16),
            pltpu.VMEM((7 * DEPTH, TILES * 2 * LANES), BF16),
            pltpu.VMEM((2, 4, ROWS, LANES), F32),
            pltpu.VMEM((TILES, 8, LANES), F32),
            pltpu.VMEM((ROWS, 2 * LANES), F32),
            pltpu.VMEM((2, POS, 16, 2 * LANES), BF16),
            pltpu.VMEM((POS + OCC, 16, 2 * LANES), BF16),
            pltpu.VMEM((POS + OCC, 16, 2 * LANES), BF16),
            pltpu.VMEM((2, 2, KB, 16, LANES), F32),
            pltpu.VMEM((2, KB, 16, LANES), F32),
            pltpu.VMEM((2, KB, 16, LANES), BF16),
            pltpu.VMEM((2, DEEP, 2, 16, LANES), BF16),
            pltpu.VMEM((2, 2, 16, LANES), F32),
            pltpu.VMEM((2, 16, LANES), F32),
            pltpu.SMEM((KC,), jnp.int32),
            pltpu.SMEM((KB,), jnp.int32),
            pltpu.SemaphoreType.REGULAR,
            pltpu.SemaphoreType.DMA,
            pltpu.SemaphoreType.DMA,
            pltpu.SemaphoreType.DMA((DEEP,)),
            pltpu.SemaphoreType.DMA,
            pltpu.SemaphoreType.DMA,
        ]
        + [pltpu.SemaphoreType.DMA((2,))] * 8
        + [pltpu.SemaphoreType.DMA((4,))],
        compiler_params=pltpu.CompilerParams(
            collective_id=0, has_side_effects=True, vmem_limit_bytes=60 * 2**20
        ),
        name="lambda_source",
    )(conserve, partner, eps_occ, eps_vir, amplitudes, integrals)


def solution(mesh):
    in_specs = (P("kb", None, None, None), P("kb", None, None, "occ", None), P(), P(), P(), P())
    out_specs = P("kb", None, ("kc", "occ"), None)
    return jax.shard_map(shards, mesh=mesh, in_specs=in_specs, out_specs=out_specs, check_vma=False)
```

```python
import functools

import jax
import jax.numpy as jnp
from jax import lax
from jax.experimental import pallas as pl
from jax.experimental.pallas import tpu as pltpu
from jax.sharding import PartitionSpec as P

KC = 8
KB = 16
OCC = 2
POS = KC * OCC
LANES = 128
PAIRS = 64
GROUPS = 8
HALF = 32
ROWS = GROUPS * HALF
DEPTH = 32
TILES = 32
CHUNK = 32
SHIFT = 2.0**-18
WIDTHS = (2 * LANES, LANES, LANES)
DEEP = 8
ORDER = (1, 7, 2, 6, 3, 5, 4)
MESH = pl.DeviceIdType.MESH
F32 = jnp.float32
BF16 = jnp.bfloat16


def place(position, kb):
    return {"kc": position // OCC, "kb": kb, "occ": position % OCC}


def kernel(
    conserve_in, partner_in, eps_occ_in, eps_vir_in, amp, slab_in, out,
    conserve, partner, eps_occ, eps_vir, slab, load_sem, abuf, symbuf, lhs, ztop, zbot, row_den, col_den, acc0, acc1,
    o1_send0, o1_send1, o1_send2, o1_recv0, o1_recv1, o1_recv2,
    o2_send0, o2_send1, o2_send2, o2_recv0, o2_recv1, o2_recv2, beta, holder, ready, copy_sem,
    h1_send, h1_recv, fwd_send, fwd_recv, h2_send, h2_recv, p1_send, p1_recv, p2_send, p2_recv,
):
    kc = lax.axis_index("kc")
    kb = lax.axis_index("kb")
    occ = lax.axis_index("occ")
    pos = kc * OCC + occ
    core = kb % 2
    z = kb // 2
    sibling = {"kb": kb + 1 - 2 * core}
    part = pos // GROUPS
    group = pos % GROUPS
    x = kc // 2
    y_lo = kc % 2
    y = occ * 2 + y_lo

    def along_z(step):
        return {"kb": (z + step) % DEEP * 2 + core}

    def along_y(step):
        to = (y + step) % 4
        return {"kc": x * 2 + to % 2, "occ": to // 2}

    acc = (acc0, acc1, acc1)
    o1_send = (o1_send0, o1_send1, o1_send2)
    o1_recv = (o1_recv0, o1_recv1, o1_recv2)
    o2_send = (o2_send0, o2_send1, o2_send2)
    o2_recv = (o2_recv0, o2_recv1, o2_recv2)
    barrier = pltpu.get_barrier_semaphore()

    own = pltpu.make_async_copy(
        amp.at[0, part, :, pl.ds(pl.multiple_of(group * LANES, LANES), LANES)],
        abuf.at[kb],
        copy_sem,
    )
    own.start()
    for step in ORDER:
        pl.semaphore_signal(barrier, inc=1, device_id=along_z(step), device_id_type=MESH)
    pl.semaphore_signal(barrier, inc=1, device_id=sibling, device_id_type=MESH)
    for step in range(1, 4):
        pl.semaphore_signal(
            barrier,
            inc=1,
            device_id={"kc": (x + step) % 4 * 2 + y_lo},
            device_id_type=MESH,
        )
        pl.semaphore_signal(barrier, inc=1, device_id=along_y(step), device_id_type=MESH)

    loads = [
        pltpu.make_async_copy(source, target, load_sem.at[at])
        for at, (source, target) in enumerate(
            (
                (slab_in, slab),
                (conserve_in, conserve),
                (partner_in, partner),
                (eps_occ_in, eps_occ),
                (eps_vir_in, eps_vir),
            )
        )
    ]
    for load in loads:
        load.start()
    own.wait()
    pl.semaphore_wait(barrier, DEEP + 6)

    def stripe_copy(step):
        return pltpu.make_async_remote_copy(
            src_ref=abuf.at[kb],
            dst_ref=abuf.at[kb],
            send_sem=h1_send,
            recv_sem=h1_recv.at[z],
            device_id=along_z(step),
            device_id_type=MESH,
        )

    def forward(label):
        pltpu.make_async_remote_copy(
            src_ref=abuf.at[label],
            dst_ref=abuf.at[label],
            send_sem=fwd_send,
            recv_sem=fwd_recv,
            device_id=sibling,
            device_id_type=MESH,
        ).start()

    for step in ORDER:
        stripe_copy(step).start()
    for step in range(1, 4):
        pl.semaphore_signal(ready, inc=1, device_id=along_y(step), device_id_type=MESH)
    forward(kb)

    ztop[...] = jnp.zeros_like(ztop)
    zbot[...] = jnp.zeros_like(zbot)
    for load in loads:
        load.wait()
    for k in range(4):
        real = slab[0, 0, :, k, :]
        imag = slab[0, 1, :, k, :]
        for u in range(8):
            at = (k * 8 + u) * 2 * LANES
            re = real[:, u * LANES : (u + 1) * LANES]
            im = imag[:, u * LANES : (u + 1) * LANES]
            ztop[3 * DEPTH : 4 * DEPTH, at : at + LANES] = re
            ztop[3 * DEPTH : 4 * DEPTH, at + LANES : at + 2 * LANES] = im
            zbot[3 * DEPTH : 4 * DEPTH, at : at + LANES] = -im
            zbot[3 * DEPTH : 4 * DEPTH, at + LANES : at + 2 * LANES] = re

    for p in range(KC):
        found = jnp.int32(0)
        for label in range(KB):
            found = found + jnp.where(conserve[label, p] == kb, label, 0)
        beta[p] = jnp.minimum(found, KB - 1)
    for label in range(KB):
        left = jnp.int32(KC)
        for p in range(KC):
            left = left - jnp.where(conserve[label, p] == kb, KC - p, 0)
        holder[label] = jnp.maximum(left, 0)
    mine = jnp.int32(0)
    for label in range(KB):
        mine = mine + jnp.where(conserve[label, kc] == kb, label, 0)
    mine = jnp.minimum(mine, KB - 1)

    row = lax.broadcasted_iota(jnp.int32, (HALF, LANES), 0)
    lane = lax.broadcasted_iota(jnp.int32, (8, LANES), 1)
    for h in range(2):
        i_of = row // 4
        j_of = (row // 2) % 2 * 4 + h * 2 + row % 2
        pair = jnp.full((HALF, LANES), -SHIFT, F32)
        for k in range(8):
            pair = pair + jnp.where(i_of == k, eps_occ[k], 0.0)
            pair = pair + jnp.where(j_of == k, eps_occ[k], 0.0)
        for a in range(DEPTH):
            g, sub = a // 4, a % 4
            row_den[h, sub, g * HALF : (g + 1) * HALF, :] = pair - eps_vir[mine, a]
    vir_c = jnp.zeros((8, LANES), F32)
    for c in range(DEPTH):
        vir_c = vir_c + jnp.where(lane % DEPTH == c, eps_vir[kb, c], 0.0)
    for u in range(8):
        vir_bc = vir_c
        for s in range(4):
            vir_bc = vir_bc + jnp.where(lane // DEPTH == s, eps_vir[kc, u * 4 + s], 0.0)
        for k in range(4):
            col_den[k * 8 + u] = eps_occ[occ * 4 + k] - vir_bc

    for landing in o1_recv:
        for zero in range(OCC):
            landing[POS + zero] = jnp.zeros(landing.shape[1:], BF16)

    out_row = lax.broadcasted_iota(jnp.int32, (PAIRS, 2 * PAIRS), 0)
    in_col = lax.broadcasted_iota(jnp.int32, (PAIRS, 2 * PAIRS), 1)
    h_of = out_row // HALF
    i_of = out_row % HALF // 4
    j_of = out_row % HALF // 2 % 2 * 4 + h_of * 2 + out_row % 2
    sign = (1 - 2 * part).astype(F32)
    order = jnp.where(in_col == i_of * 8 + j_of, 1.0, 0.0) + jnp.where(
        in_col == PAIRS + j_of * 8 + i_of, sign, 0.0
    )
    order = order.astype(BF16)

    perm_row = lax.broadcasted_iota(jnp.int32, (ROWS, ROWS), 0)
    perm_col = lax.broadcasted_iota(jnp.int32, (ROWS, ROWS), 1)
    perm_from = perm_row % 16 // 2 * HALF + perm_row // 16 * 2 + perm_row % 2
    perm = jnp.where(perm_col == perm_from, 1.0, 0.0).astype(BF16)

    for step in ORDER:
        came = (z + DEEP - step) % DEEP
        pltpu.make_async_remote_copy(
            src_ref=abuf.at[kb],
            dst_ref=abuf.at[kb],
            send_sem=h1_send,
            recv_sem=h1_recv.at[came],
            device_id=sibling,
            device_id_type=MESH,
        ).wait_recv()
        forward(came * 2 + core)
    forwarded = pltpu.make_async_remote_copy(
        src_ref=abuf.at[pl.ds(0, DEEP)],
        dst_ref=abuf.at[pl.ds(0, DEEP)],
        send_sem=fwd_send,
        recv_sem=fwd_recv,
        device_id=sibling,
        device_id_type=MESH,
    )
    forwarded.wait_recv()
    pl.semaphore_wait(ready, 3)
    for p in range(KC):
        label = beta[p]
        both = jnp.concatenate([abuf[label], abuf[partner[label]]], axis=0)
        sym = jnp.dot(order, both, preferred_element_type=F32).astype(BF16)
        symbuf[0, p] = sym[:HALF]
        symbuf[1, p] = sym[HALF:]
    def send_rows(h):
        lhs[h, pos] = symbuf[h, kc]

        @pl.loop(1, POS)
        def _(step):
            to = (pos + step) % POS
            pltpu.make_async_remote_copy(
                src_ref=symbuf.at[h, to // OCC],
                dst_ref=lhs.at[h, pos],
                send_sem=h2_send.at[h],
                recv_sem=h2_recv.at[h],
                device_id=place(to, kb),
                device_id_type=MESH,
            ).start()

    def lhs_wait(h):
        return pltpu.make_async_remote_copy(
            src_ref=lhs.at[h, pl.ds(0, POS - 1)],
            dst_ref=lhs.at[h, pl.ds(0, POS - 1)],
            send_sem=h2_send.at[h],
            recv_sem=h2_recv.at[h],
            device_id=sibling,
            device_id_type=MESH,
        )

    def multiply(unit, h, first, last):
        acc[unit][...] = jnp.zeros_like(acc[unit])
        left = jnp.concatenate(
            [
                lhs[h, 0:GROUPS].reshape(ROWS, LANES),
                lhs[h, GROUPS:POS].reshape(ROWS, LANES),
            ],
            axis=1,
        )

        @pl.loop(first, last)
        def _(step):
            sub = step // (TILES // CHUNK)
            chunk = step % (TILES // CHUNK)
            at = pl.multiple_of(chunk * (CHUNK * 2 * LANES), CHUNK * 2 * LANES)
            down = pl.multiple_of((3 - sub) * DEPTH, DEPTH)
            weight = jnp.concatenate(
                [
                    ztop[pl.ds(down, 4 * DEPTH), pl.ds(at, CHUNK * 2 * LANES)],
                    zbot[pl.ds(down, 4 * DEPTH), pl.ds(at, CHUNK * 2 * LANES)],
                ],
                axis=0,
            )
            product = jnp.dot(left, weight, preferred_element_type=F32)
            den_row = row_den[h, sub]
            parts = []
            for s in range(CHUNK):
                den = den_row + col_den[chunk * CHUNK + s, 0:1, :]
                inverse = jnp.clip(pltpu.reciprocal(den, approx=True), -1.0, 1.0)
                lo = s * 2 * LANES
                parts.append((product[:, lo : lo + LANES] * inverse).astype(BF16))
                parts.append((product[:, lo + LANES : lo + 2 * LANES] * inverse).astype(BF16))
            scaled = jnp.concatenate(parts, axis=1)
            if unit == 0:
                back = weight
            else:
                near = pl.multiple_of((3 - sub % 2) * DEPTH, DEPTH)
                back = jnp.concatenate(
                    [
                        ztop[pl.ds(near, 2 * DEPTH), pl.ds(at, CHUNK * 2 * LANES)],
                        zbot[pl.ds(near, 2 * DEPTH), pl.ds(at, CHUNK * 2 * LANES)],
                    ],
                    axis=0,
                )
            acc[unit][...] += lax.dot_general(
                scaled, back, (((1,), (1,)), ((), ())), preferred_element_type=F32
            )

    def send_partials(unit):
        sums = acc[unit][...].astype(BF16)
        packed = jnp.dot(perm, sums, preferred_element_type=F32).astype(BF16)
        for r in range(POS):
            o1_send[unit][r] = packed[r * 16 : (r + 1) * 16]
        o1_recv[unit][pos] = o1_send[unit][pos]

        @pl.loop(1, POS)
        def _(step):
            to = (pos + step) % POS
            pltpu.make_async_remote_copy(
                src_ref=o1_send[unit].at[to],
                dst_ref=o1_recv[unit].at[pos],
                send_sem=p1_send.at[unit],
                recv_sem=p1_recv.at[unit],
                device_id=place(to, kb),
                device_id_type=MESH,
            ).start()

    def partials_wait(unit):
        return pltpu.make_async_remote_copy(
            src_ref=o1_send[unit].at[pl.ds(0, POS - 1)],
            dst_ref=o1_recv[unit].at[pl.ds(0, POS - 1)],
            send_sem=p1_send.at[unit],
            recv_sem=p1_recv.at[unit],
            device_id=sibling,
            device_id_type=MESH,
        )

    def send_sums(unit):
        partials_wait(unit).wait_recv()
        for label in range(KB):
            at = holder[label] * OCC
            total = o1_recv[unit][at].astype(F32) + o1_recv[unit][at + 1].astype(F32)
            o2_send[unit][label] = total.astype(BF16)
        o2_recv[unit][kb] = o2_send[unit][kb]

        @pl.loop(1, KB)
        def _(step):
            to = (kb + step) % KB
            pltpu.make_async_remote_copy(
                src_ref=o2_send[unit].at[to],
                dst_ref=o2_recv[unit].at[kb],
                send_sem=p2_send.at[unit],
                recv_sem=p2_recv.at[unit],
                device_id={"kb": to},
                device_id_type=MESH,
            ).start()

    def sums_wait(unit):
        return pltpu.make_async_remote_copy(
            src_ref=o2_send[unit].at[pl.ds(0, KB - 1)],
            dst_ref=o2_recv[unit].at[pl.ds(0, KB - 1)],
            send_sem=p2_send.at[unit],
            recv_sem=p2_recv.at[unit],
            device_id=sibling,
            device_id_type=MESH,
        )

    def total_of(unit):
        sums_wait(unit).wait_recv()
        total = o2_recv[unit][0].astype(F32)
        for label in range(1, KB):
            total = total + o2_recv[unit][label].astype(F32)
        return total

    def finish(h, parts):
        for c in range(2):
            for g in range(GROUPS):
                out[0, c, 2 * h : 2 * h + 2, g * LANES : (g + 1) * LANES] = parts[c][
                    2 * g : 2 * g + 2
                ]

    steps = 4 * TILES // CHUNK
    half = steps // 2
    send_rows(0)
    lhs_wait(0).wait_recv()
    send_rows(1)
    multiply(0, 0, 0, steps)
    send_partials(0)
    lhs_wait(1).wait_recv()
    multiply(1, 1, 0, half)
    send_partials(1)
    send_sums(0)
    multiply(2, 1, half, steps)
    send_partials(2)
    send_sums(1)
    whole = total_of(0)
    finish(0, (whole[:, :LANES], whole[:, LANES:]))
    send_sums(2)
    pltpu.make_async_remote_copy(
        src_ref=abuf.at[pl.ds(0, DEEP - 1)],
        dst_ref=abuf.at[pl.ds(0, DEEP - 1)],
        send_sem=h1_send,
        recv_sem=fwd_recv,
        device_id=sibling,
        device_id_type=MESH,
    ).wait_send()
    forwarded.wait_send()
    for h in range(2):
        lhs_wait(h).wait_send()
    for unit in range(3):
        partials_wait(unit).wait_send()
    lane = lax.broadcasted_iota(jnp.int32, (16, LANES), 1)
    first = total_of(1)
    second = total_of(2)
    finish(
        1,
        (
            jnp.where(lane < 64, first, pltpu.roll(second, 64, 1)),
            jnp.where(lane < 64, pltpu.roll(first, 64, 1), second),
        ),
    )
    for unit in range(3):
        sums_wait(unit).wait_send()


def shards(amplitudes, integrals, eps_occ, eps_vir, conserve, partner):
    return pl.pallas_call(
        kernel,
        out_shape=jax.ShapeDtypeStruct((1, 2, 4, GROUPS * LANES), F32),
        in_specs=[pl.BlockSpec(memory_space=pl.ANY)] * 6,
        out_specs=pl.BlockSpec(memory_space=pltpu.VMEM),
        scratch_shapes=[
            pltpu.SMEM((KB, KB), jnp.int32),
            pltpu.SMEM((KB,), jnp.int32),
            pltpu.SMEM((8,), F32),
            pltpu.SMEM((KB, DEPTH), F32),
            pltpu.VMEM((1, 2, DEPTH, 4, 1024), BF16),
            pltpu.SemaphoreType.DMA((5,)),
            pltpu.VMEM((KB, PAIRS, LANES), BF16),
            pltpu.VMEM((2, KC, HALF, LANES), BF16),
            pltpu.VMEM((2, POS, HALF, LANES), BF16),
            pltpu.VMEM((7 * DEPTH, TILES * 2 * LANES), BF16),
            pltpu.VMEM((7 * DEPTH, TILES * 2 * LANES), BF16),
            pltpu.VMEM((2, 4, ROWS, LANES), F32),
            pltpu.VMEM((TILES, 8, LANES), F32),
            pltpu.VMEM((ROWS, 2 * LANES), F32),
            pltpu.VMEM((ROWS, LANES), F32),
        ]
        + [pltpu.VMEM((POS, 16, width), BF16) for width in WIDTHS]
        + [pltpu.VMEM((POS + OCC, 16, width), BF16) for width in WIDTHS]
        + [pltpu.VMEM((KB, 16, width), BF16) for width in WIDTHS] * 2
        + [
            pltpu.SMEM((KC,), jnp.int32),
            pltpu.SMEM((KB,), jnp.int32),
            pltpu.SemaphoreType.REGULAR,
            pltpu.SemaphoreType.DMA,
            pltpu.SemaphoreType.DMA,
            pltpu.SemaphoreType.DMA((DEEP,)),
            pltpu.SemaphoreType.DMA,
            pltpu.SemaphoreType.DMA,
        ]
        + [pltpu.SemaphoreType.DMA((2,))] * 2
        + [pltpu.SemaphoreType.DMA((3,))] * 4,
        compiler_params=pltpu.CompilerParams(
            collective_id=0, has_side_effects=True, vmem_limit_bytes=60 * 2**20
        ),
        name="lambda_source",
    )(conserve, partner, eps_occ, eps_vir, amplitudes, integrals)


def solution(mesh):
    in_specs = (P("kb", None, None, None), P("kb", None, None, "occ", None), P(), P(), P(), P())
    out_specs = P("kb", None, ("kc", "occ"), None)
    return jax.shard_map(shards, mesh=mesh, in_specs=in_specs, out_specs=out_specs, check_vma=False)
```

```python
import functools

import jax
import jax.numpy as jnp
from jax import lax
from jax.experimental import pallas as pl
from jax.experimental.pallas import tpu as pltpu
from jax.sharding import PartitionSpec as P

KC = 8
KB = 16
OCC = 2
POS = KC * OCC
LANES = 128
PAIRS = 64
GROUPS = 8
HALF = 32
ROWS = GROUPS * HALF
DEPTH = 32
TILES = 32
CHUNK = 32
SHIFT = 2.0**-18
WIDTHS = (2 * LANES, LANES, LANES)
DEEP = 8
ORDER = (1, 7, 2, 6, 3, 5, 4)
MESH = pl.DeviceIdType.MESH
F32 = jnp.float32
BF16 = jnp.bfloat16


def place(position, kb):
    return {"kc": position // OCC, "kb": kb, "occ": position % OCC}


def kernel(
    conserve_in, partner_in, eps_occ_in, eps_vir_in, amp, slab_in, out,
    conserve, partner, eps_occ, eps_vir, slab, load_sem, abuf, symbuf, lhs, ztop, zbot, row_den, col_den, acc0, acc1,
    o1_send0, o1_send1, o1_send2, o1_recv0, o1_recv1, o1_recv2,
    o2_send0, o2_send1, o2_send2, o2_recv0, o2_recv1, o2_recv2, beta, holder, ready, copy_sem,
    h1_send, h1_recv, fwd_send, fwd_recv, h2_send, h2_recv, p1_send, p1_recv, p2_send, p2_recv,
):
    kc = lax.axis_index("kc")
    kb = lax.axis_index("kb")
    occ = lax.axis_index("occ")
    pos = kc * OCC + occ
    core = kb % 2
    z = kb // 2
    sibling = {"kb": kb + 1 - 2 * core}
    part = pos // GROUPS
    group = pos % GROUPS
    x = kc // 2
    y_lo = kc % 2
    y = occ * 2 + y_lo

    def along_z(step):
        return {"kb": (z + step) % DEEP * 2 + core}

    def along_y(step):
        to = (y + step) % 4
        return {"kc": x * 2 + to % 2, "occ": to // 2}

    acc = (acc0, acc1, acc1)
    o1_send = (o1_send0, o1_send1, o1_send2)
    o1_recv = (o1_recv0, o1_recv1, o1_recv2)
    o2_send = (o2_send0, o2_send1, o2_send2)
    o2_recv = (o2_recv0, o2_recv1, o2_recv2)
    barrier = pltpu.get_barrier_semaphore()

    own = pltpu.make_async_copy(
        amp.at[0, part, :, pl.ds(pl.multiple_of(group * LANES, LANES), LANES)],
        abuf.at[kb],
        copy_sem,
    )
    own.start()
    for step in ORDER:
        pl.semaphore_signal(barrier, inc=1, device_id=along_z(step), device_id_type=MESH)
    pl.semaphore_signal(barrier, inc=1, device_id=sibling, device_id_type=MESH)
    for step in range(1, 4):
        pl.semaphore_signal(
            barrier,
            inc=1,
            device_id={"kc": (x + step) % 4 * 2 + y_lo},
            device_id_type=MESH,
        )
        pl.semaphore_signal(barrier, inc=1, device_id=along_y(step), device_id_type=MESH)

    loads = [
        pltpu.make_async_copy(source, target, load_sem.at[at])
        for at, (source, target) in enumerate(
            (
                (slab_in, slab),
                (conserve_in, conserve),
                (partner_in, partner),
                (eps_occ_in, eps_occ),
                (eps_vir_in, eps_vir),
            )
        )
    ]
    for load in loads:
        load.start()
    own.wait()
    pl.semaphore_wait(barrier, DEEP + 6)

    def stripe_copy(step):
        return pltpu.make_async_remote_copy(
            src_ref=abuf.at[kb],
            dst_ref=abuf.at[kb],
            send_sem=h1_send,
            recv_sem=h1_recv.at[z],
            device_id=along_z(step),
            device_id_type=MESH,
        )

    def forward(label):
        pltpu.make_async_remote_copy(
            src_ref=abuf.at[label],
            dst_ref=abuf.at[label],
            send_sem=fwd_send,
            recv_sem=fwd_recv,
            device_id=sibling,
            device_id_type=MESH,
        ).start()

    for step in ORDER:
        stripe_copy(step).start()
    for step in range(1, 4):
        pl.semaphore_signal(ready, inc=1, device_id=along_y(step), device_id_type=MESH)
    forward(kb)

    ztop[...] = jnp.zeros_like(ztop)
    zbot[...] = jnp.zeros_like(zbot)
    for load in loads:
        load.wait()
    for k in range(4):
        real = slab[0, 0, :, k, :]
        imag = slab[0, 1, :, k, :]
        for u in range(8):
            at = (k * 8 + u) * 2 * LANES
            re = real[:, u * LANES : (u + 1) * LANES]
            im = imag[:, u * LANES : (u + 1) * LANES]
            ztop[3 * DEPTH : 4 * DEPTH, at : at + LANES] = re
            ztop[3 * DEPTH : 4 * DEPTH, at + LANES : at + 2 * LANES] = im
            zbot[3 * DEPTH : 4 * DEPTH, at : at + LANES] = -im
            zbot[3 * DEPTH : 4 * DEPTH, at + LANES : at + 2 * LANES] = re

    for p in range(KC):
        found = jnp.int32(0)
        for label in range(KB):
            found = found + jnp.where(conserve[label, p] == kb, label, 0)
        beta[p] = jnp.minimum(found, KB - 1)
    for label in range(KB):
        left = jnp.int32(KC)
        for p in range(KC):
            left = left - jnp.where(conserve[label, p] == kb, KC - p, 0)
        holder[label] = jnp.maximum(left, 0)
    mine = jnp.int32(0)
    for label in range(KB):
        mine = mine + jnp.where(conserve[label, kc] == kb, label, 0)
    mine = jnp.minimum(mine, KB - 1)

    row = lax.broadcasted_iota(jnp.int32, (HALF, LANES), 0)
    lane = lax.broadcasted_iota(jnp.int32, (8, LANES), 1)
    for h in range(2):
        i_of = row // 4
        j_of = (row // 2) % 2 * 4 + h * 2 + row % 2
        pair = jnp.full((HALF, LANES), -SHIFT, F32)
        for k in range(8):
            pair = pair + jnp.where(i_of == k, eps_occ[k], 0.0)
            pair = pair + jnp.where(j_of == k, eps_occ[k], 0.0)
        for a in range(DEPTH):
            g, sub = a // 4, a % 4
            row_den[h, sub, g * HALF : (g + 1) * HALF, :] = pair - eps_vir[mine, a]
    vir_c = jnp.zeros((8, LANES), F32)
    for c in range(DEPTH):
        vir_c = vir_c + jnp.where(lane % DEPTH == c, eps_vir[kb, c], 0.0)
    for u in range(8):
        vir_bc = vir_c
        for s in range(4):
            vir_bc = vir_bc + jnp.where(lane // DEPTH == s, eps_vir[kc, u * 4 + s], 0.0)
        for k in range(4):
            col_den[k * 8 + u] = eps_occ[occ * 4 + k] - vir_bc

    for landing in o1_recv:
        for zero in range(OCC):
            landing[POS + zero] = jnp.zeros(landing.shape[1:], BF16)

    out_row = lax.broadcasted_iota(jnp.int32, (PAIRS, 2 * PAIRS), 0)
    in_col = lax.broadcasted_iota(jnp.int32, (PAIRS, 2 * PAIRS), 1)
    h_of = out_row // HALF
    i_of = out_row % HALF // 4
    j_of = out_row % HALF // 2 % 2 * 4 + h_of * 2 + out_row % 2
    sign = (1 - 2 * part).astype(F32)
    order = jnp.where(in_col == i_of * 8 + j_of, 1.0, 0.0) + jnp.where(
        in_col == PAIRS + j_of * 8 + i_of, sign, 0.0
    )
    order = order.astype(BF16)

    perm_row = lax.broadcasted_iota(jnp.int32, (ROWS, ROWS), 0)
    perm_col = lax.broadcasted_iota(jnp.int32, (ROWS, ROWS), 1)
    perm_from = perm_row % 16 // 2 * HALF + perm_row // 16 * 2 + perm_row % 2
    perm = jnp.where(perm_col == perm_from, 1.0, 0.0).astype(BF16)

    for step in ORDER:
        came = (z + DEEP - step) % DEEP
        pltpu.make_async_remote_copy(
            src_ref=abuf.at[kb],
            dst_ref=abuf.at[kb],
            send_sem=h1_send,
            recv_sem=h1_recv.at[came],
            device_id=sibling,
            device_id_type=MESH,
        ).wait_recv()
        forward(came * 2 + core)
    forwarded = pltpu.make_async_remote_copy(
        src_ref=abuf.at[pl.ds(0, DEEP)],
        dst_ref=abuf.at[pl.ds(0, DEEP)],
        send_sem=fwd_send,
        recv_sem=fwd_recv,
        device_id=sibling,
        device_id_type=MESH,
    )
    forwarded.wait_recv()
    pl.semaphore_wait(ready, 3)
    for p in range(KC):
        label = beta[p]
        both = jnp.concatenate([abuf[label], abuf[partner[label]]], axis=0)
        sym = jnp.dot(order, both, preferred_element_type=F32).astype(BF16)
        symbuf[0, p] = sym[:HALF]
        symbuf[1, p] = sym[HALF:]
    def send_rows(h):
        lhs[h, pos] = symbuf[h, kc]

        @pl.loop(1, POS)
        def _(step):
            to = (pos + step) % POS
            pltpu.make_async_remote_copy(
                src_ref=symbuf.at[h, to // OCC],
                dst_ref=lhs.at[h, pos],
                send_sem=h2_send.at[h],
                recv_sem=h2_recv.at[h],
                device_id=place(to, kb),
                device_id_type=MESH,
            ).start()

    def lhs_wait(h):
        return pltpu.make_async_remote_copy(
            src_ref=lhs.at[h, pl.ds(0, POS - 1)],
            dst_ref=lhs.at[h, pl.ds(0, POS - 1)],
            send_sem=h2_send.at[h],
            recv_sem=h2_recv.at[h],
            device_id=sibling,
            device_id_type=MESH,
        )

    def multiply(unit, h, first, last):
        acc[unit][...] = jnp.zeros_like(acc[unit])
        left = jnp.concatenate(
            [
                lhs[h, 0:GROUPS].reshape(ROWS, LANES),
                lhs[h, GROUPS:POS].reshape(ROWS, LANES),
            ],
            axis=1,
        )

        @pl.loop(first, last, unroll=2 if unit == 0 else 1)
        def _(step):
            sub = step // (TILES // CHUNK)
            chunk = step % (TILES // CHUNK)
            at = pl.multiple_of(chunk * (CHUNK * 2 * LANES), CHUNK * 2 * LANES)
            down = pl.multiple_of((3 - sub) * DEPTH, DEPTH)
            weight = jnp.concatenate(
                [
                    ztop[pl.ds(down, 4 * DEPTH), pl.ds(at, CHUNK * 2 * LANES)],
                    zbot[pl.ds(down, 4 * DEPTH), pl.ds(at, CHUNK * 2 * LANES)],
                ],
                axis=0,
            )
            product = jnp.dot(left, weight, preferred_element_type=F32)
            den_row = row_den[h, sub]
            parts = []
            for s in range(CHUNK):
                den = den_row + col_den[chunk * CHUNK + s, 0:1, :]
                inverse = jnp.clip(pltpu.reciprocal(den, approx=True), -1.0, 1.0)
                lo = s * 2 * LANES
                parts.append((product[:, lo : lo + LANES] * inverse).astype(BF16))
                parts.append((product[:, lo + LANES : lo + 2 * LANES] * inverse).astype(BF16))
            scaled = jnp.concatenate(parts, axis=1)
            if unit == 0:
                back = weight
            else:
                near = pl.multiple_of((3 - sub % 2) * DEPTH, DEPTH)
                back = jnp.concatenate(
                    [
                        ztop[pl.ds(near, 2 * DEPTH), pl.ds(at, CHUNK * 2 * LANES)],
                        zbot[pl.ds(near, 2 * DEPTH), pl.ds(at, CHUNK * 2 * LANES)],
                    ],
                    axis=0,
                )
            acc[unit][...] += lax.dot_general(
                scaled, back, (((1,), (1,)), ((), ())), preferred_element_type=F32
            )

    def send_partials(unit):
        sums = acc[unit][...].astype(BF16)
        packed = jnp.dot(perm, sums, preferred_element_type=F32).astype(BF16)
        for r in range(POS):
            o1_send[unit][r] = packed[r * 16 : (r + 1) * 16]
        o1_recv[unit][pos] = o1_send[unit][pos]

        @pl.loop(1, POS)
        def _(step):
            to = (pos + step) % POS
            pltpu.make_async_remote_copy(
                src_ref=o1_send[unit].at[to],
                dst_ref=o1_recv[unit].at[pos],
                send_sem=p1_send.at[unit],
                recv_sem=p1_recv.at[unit],
                device_id=place(to, kb),
                device_id_type=MESH,
            ).start()

    def partials_wait(unit):
        return pltpu.make_async_remote_copy(
            src_ref=o1_send[unit].at[pl.ds(0, POS - 1)],
            dst_ref=o1_recv[unit].at[pl.ds(0, POS - 1)],
            send_sem=p1_send.at[unit],
            recv_sem=p1_recv.at[unit],
            device_id=sibling,
            device_id_type=MESH,
        )

    def send_sums(unit):
        partials_wait(unit).wait_recv()
        for label in range(KB):
            at = holder[label] * OCC
            total = o1_recv[unit][at].astype(F32) + o1_recv[unit][at + 1].astype(F32)
            o2_send[unit][label] = total.astype(BF16)
        o2_recv[unit][kb] = o2_send[unit][kb]

        @pl.loop(1, KB)
        def _(step):
            to = (kb + step) % KB
            pltpu.make_async_remote_copy(
                src_ref=o2_send[unit].at[to],
                dst_ref=o2_recv[unit].at[kb],
                send_sem=p2_send.at[unit],
                recv_sem=p2_recv.at[unit],
                device_id={"kb": to},
                device_id_type=MESH,
            ).start()

    def sums_wait(unit):
        return pltpu.make_async_remote_copy(
            src_ref=o2_send[unit].at[pl.ds(0, KB - 1)],
            dst_ref=o2_recv[unit].at[pl.ds(0, KB - 1)],
            send_sem=p2_send.at[unit],
            recv_sem=p2_recv.at[unit],
            device_id=sibling,
            device_id_type=MESH,
        )

    def total_of(unit):
        sums_wait(unit).wait_recv()
        total = o2_recv[unit][0].astype(F32)
        for label in range(1, KB):
            total = total + o2_recv[unit][label].astype(F32)
        return total

    def finish(h, parts):
        for c in range(2):
            for g in range(GROUPS):
                out[0, c, 2 * h : 2 * h + 2, g * LANES : (g + 1) * LANES] = parts[c][
                    2 * g : 2 * g + 2
                ]

    steps = 4 * TILES // CHUNK
    half = steps // 2
    send_rows(0)
    lhs_wait(0).wait_recv()
    send_rows(1)
    multiply(0, 0, 0, steps)
    send_partials(0)
    lhs_wait(1).wait_recv()
    multiply(1, 1, 0, half)
    send_partials(1)
    send_sums(0)
    multiply(2, 1, half, steps)
    send_partials(2)
    send_sums(1)
    whole = total_of(0)
    finish(0, (whole[:, :LANES], whole[:, LANES:]))
    send_sums(2)
    pltpu.make_async_remote_copy(
        src_ref=abuf.at[pl.ds(0, DEEP - 1)],
        dst_ref=abuf.at[pl.ds(0, DEEP - 1)],
        send_sem=h1_send,
        recv_sem=fwd_recv,
        device_id=sibling,
        device_id_type=MESH,
    ).wait_send()
    forwarded.wait_send()
    for h in range(2):
        lhs_wait(h).wait_send()
    for unit in range(3):
        partials_wait(unit).wait_send()
    lane = lax.broadcasted_iota(jnp.int32, (16, LANES), 1)
    first = total_of(1)
    second = total_of(2)
    finish(
        1,
        (
            jnp.where(lane < 64, first, pltpu.roll(second, 64, 1)),
            jnp.where(lane < 64, pltpu.roll(first, 64, 1), second),
        ),
    )
    for unit in range(3):
        sums_wait(unit).wait_send()


def shards(amplitudes, integrals, eps_occ, eps_vir, conserve, partner):
    return pl.pallas_call(
        kernel,
        out_shape=jax.ShapeDtypeStruct((1, 2, 4, GROUPS * LANES), F32),
        in_specs=[pl.BlockSpec(memory_space=pl.ANY)] * 6,
        out_specs=pl.BlockSpec(memory_space=pltpu.VMEM),
        scratch_shapes=[
            pltpu.SMEM((KB, KB), jnp.int32),
            pltpu.SMEM((KB,), jnp.int32),
            pltpu.SMEM((8,), F32),
            pltpu.SMEM((KB, DEPTH), F32),
            pltpu.VMEM((1, 2, DEPTH, 4, 1024), BF16),
            pltpu.SemaphoreType.DMA((5,)),
            pltpu.VMEM((KB, PAIRS, LANES), BF16),
            pltpu.VMEM((2, KC, HALF, LANES), BF16),
            pltpu.VMEM((2, POS, HALF, LANES), BF16),
            pltpu.VMEM((7 * DEPTH, TILES * 2 * LANES), BF16),
            pltpu.VMEM((7 * DEPTH, TILES * 2 * LANES), BF16),
            pltpu.VMEM((2, 4, ROWS, LANES), F32),
            pltpu.VMEM((TILES, 8, LANES), F32),
            pltpu.VMEM((ROWS, 2 * LANES), F32),
            pltpu.VMEM((ROWS, LANES), F32),
        ]
        + [pltpu.VMEM((POS, 16, width), BF16) for width in WIDTHS]
        + [pltpu.VMEM((POS + OCC, 16, width), BF16) for width in WIDTHS]
        + [pltpu.VMEM((KB, 16, width), BF16) for width in WIDTHS] * 2
        + [
            pltpu.SMEM((KC,), jnp.int32),
            pltpu.SMEM((KB,), jnp.int32),
            pltpu.SemaphoreType.REGULAR,
            pltpu.SemaphoreType.DMA,
            pltpu.SemaphoreType.DMA,
            pltpu.SemaphoreType.DMA((DEEP,)),
            pltpu.SemaphoreType.DMA,
            pltpu.SemaphoreType.DMA,
        ]
        + [pltpu.SemaphoreType.DMA((2,))] * 2
        + [pltpu.SemaphoreType.DMA((3,))] * 4,
        compiler_params=pltpu.CompilerParams(
            collective_id=0, has_side_effects=True, vmem_limit_bytes=60 * 2**20
        ),
        name="lambda_source",
    )(conserve, partner, eps_occ, eps_vir, amplitudes, integrals)


def solution(mesh):
    in_specs = (P("kb", None, None, None), P("kb", None, None, "occ", None), P(), P(), P(), P())
    out_specs = P("kb", None, ("kc", "occ"), None)
    return jax.shard_map(shards, mesh=mesh, in_specs=in_specs, out_specs=out_specs, check_vma=False)
```

```python
import functools

import jax
import jax.numpy as jnp
from jax import lax
from jax.experimental import pallas as pl
from jax.experimental.pallas import tpu as pltpu
from jax.sharding import PartitionSpec as P

KC = 8
KB = 16
OCC = 2
POS = KC * OCC
LANES = 128
PAIRS = 64
GROUPS = 8
HALF = 32
ROWS = GROUPS * HALF
DEPTH = 32
TILES = 32
CHUNK = 32
SHIFT = 2.0**-18
WIDTHS = (2 * LANES, LANES, LANES)
DEEP = 8
ORDER = (1, 7, 2, 6, 3, 5, 4)
MESH = pl.DeviceIdType.MESH
F32 = jnp.float32
BF16 = jnp.bfloat16


def place(position, kb):
    return {"kc": position // OCC, "kb": kb, "occ": position % OCC}


def kernel(
    conserve_in, partner_in, eps_occ_in, eps_vir_in, amp, slab_in, out,
    conserve, partner, eps_occ, eps_vir, slab, load_sem, abuf, symbuf, lhs, ztop, zbot, row_den, col_den, acc0, acc1,
    o1_send0, o1_send1, o1_send2, o1_recv0, o1_recv1, o1_recv2,
    o2_send0, o2_send1, o2_send2, o2_recv0, o2_recv1, o2_recv2, beta, holder, ready, copy_sem,
    h1_send, h1_recv, fwd_send, fwd_recv, h2_send, h2_recv, p1_send, p1_recv, p2_send, p2_recv,
):
    kc = lax.axis_index("kc")
    kb = lax.axis_index("kb")
    occ = lax.axis_index("occ")
    pos = kc * OCC + occ
    core = kb % 2
    z = kb // 2
    sibling = {"kb": kb + 1 - 2 * core}
    part = pos // GROUPS
    group = pos % GROUPS
    x = kc // 2
    y_lo = kc % 2
    y = occ * 2 + y_lo

    def along_z(step):
        return {"kb": (z + step) % DEEP * 2 + core}

    def along_y(step):
        to = (y + step) % 4
        return {"kc": x * 2 + to % 2, "occ": to // 2}

    acc = (acc0, acc1, acc1)
    o1_send = (o1_send0, o1_send1, o1_send2)
    o1_recv = (o1_recv0, o1_recv1, o1_recv2)
    o2_send = (o2_send0, o2_send1, o2_send2)
    o2_recv = (o2_recv0, o2_recv1, o2_recv2)
    barrier = pltpu.get_barrier_semaphore()

    own = pltpu.make_async_copy(
        amp.at[0, part, :, pl.ds(pl.multiple_of(group * LANES, LANES), LANES)],
        abuf.at[kb],
        copy_sem,
    )
    own.start()
    for step in ORDER:
        pl.semaphore_signal(barrier, inc=1, device_id=along_z(step), device_id_type=MESH)
    pl.semaphore_signal(barrier, inc=1, device_id=sibling, device_id_type=MESH)
    for step in range(1, 4):
        pl.semaphore_signal(
            barrier,
            inc=1,
            device_id={"kc": (x + step) % 4 * 2 + y_lo},
            device_id_type=MESH,
        )
        pl.semaphore_signal(barrier, inc=1, device_id=along_y(step), device_id_type=MESH)

    loads = [
        pltpu.make_async_copy(source, target, load_sem.at[at])
        for at, (source, target) in enumerate(
            (
                (slab_in, slab),
                (conserve_in, conserve),
                (partner_in, partner),
                (eps_occ_in, eps_occ),
                (eps_vir_in, eps_vir),
            )
        )
    ]
    for load in loads:
        load.start()
    own.wait()
    pl.semaphore_wait(barrier, DEEP + 6)

    def stripe_copy(step):
        return pltpu.make_async_remote_copy(
            src_ref=abuf.at[kb],
            dst_ref=abuf.at[kb],
            send_sem=h1_send,
            recv_sem=h1_recv.at[z],
            device_id=along_z(step),
            device_id_type=MESH,
        )

    def forward(label):
        pltpu.make_async_remote_copy(
            src_ref=abuf.at[label],
            dst_ref=abuf.at[label],
            send_sem=fwd_send,
            recv_sem=fwd_recv,
            device_id=sibling,
            device_id_type=MESH,
        ).start()

    for step in ORDER:
        stripe_copy(step).start()
    for step in range(1, 4):
        pl.semaphore_signal(ready, inc=1, device_id=along_y(step), device_id_type=MESH)
    forward(kb)

    ztop[...] = jnp.zeros_like(ztop)
    zbot[...] = jnp.zeros_like(zbot)
    for load in loads:
        load.wait()
    for k in range(4):
        real = slab[0, 0, :, k, :]
        imag = slab[0, 1, :, k, :]
        for u in range(8):
            at = (k * 8 + u) * 2 * LANES
            re = real[:, u * LANES : (u + 1) * LANES]
            im = imag[:, u * LANES : (u + 1) * LANES]
            ztop[3 * DEPTH : 4 * DEPTH, at : at + LANES] = re
            ztop[3 * DEPTH : 4 * DEPTH, at + LANES : at + 2 * LANES] = im
            zbot[3 * DEPTH : 4 * DEPTH, at : at + LANES] = -im
            zbot[3 * DEPTH : 4 * DEPTH, at + LANES : at + 2 * LANES] = re

    for p in range(KC):
        found = jnp.int32(0)
        for label in range(KB):
            found = found + jnp.where(conserve[label, p] == kb, label, 0)
        beta[p] = jnp.minimum(found, KB - 1)
    for label in range(KB):
        left = jnp.int32(KC)
        for p in range(KC):
            left = left - jnp.where(conserve[label, p] == kb, KC - p, 0)
        holder[label] = jnp.maximum(left, 0)
    mine = jnp.int32(0)
    for label in range(KB):
        mine = mine + jnp.where(conserve[label, kc] == kb, label, 0)
    mine = jnp.minimum(mine, KB - 1)

    row = lax.broadcasted_iota(jnp.int32, (HALF, LANES), 0)
    lane = lax.broadcasted_iota(jnp.int32, (8, LANES), 1)
    for h in range(2):
        i_of = row // 4
        j_of = (row // 2) % 2 * 4 + h * 2 + row % 2
        pair = jnp.full((HALF, LANES), -SHIFT, F32)
        for k in range(8):
            pair = pair + jnp.where(i_of == k, eps_occ[k], 0.0)
            pair = pair + jnp.where(j_of == k, eps_occ[k], 0.0)
        for a in range(DEPTH):
            g, sub = a // 4, a % 4
            row_den[h, sub, g * HALF : (g + 1) * HALF, :] = pair - eps_vir[mine, a]
    vir_c = jnp.zeros((8, LANES), F32)
    for c in range(DEPTH):
        vir_c = vir_c + jnp.where(lane % DEPTH == c, eps_vir[kb, c], 0.0)
    for u in range(8):
        vir_bc = vir_c
        for s in range(4):
            vir_bc = vir_bc + jnp.where(lane // DEPTH == s, eps_vir[kc, u * 4 + s], 0.0)
        for k in range(4):
            col_den[k * 8 + u] = eps_occ[occ * 4 + k] - vir_bc

    for landing in o1_recv:
        for zero in range(OCC):
            landing[POS + zero] = jnp.zeros(landing.shape[1:], BF16)

    out_row = lax.broadcasted_iota(jnp.int32, (PAIRS, 2 * PAIRS), 0)
    in_col = lax.broadcasted_iota(jnp.int32, (PAIRS, 2 * PAIRS), 1)
    h_of = out_row // HALF
    i_of = out_row % HALF // 4
    j_of = out_row % HALF // 2 % 2 * 4 + h_of * 2 + out_row % 2
    sign = (1 - 2 * part).astype(F32)
    order = jnp.where(in_col == i_of * 8 + j_of, 1.0, 0.0) + jnp.where(
        in_col == PAIRS + j_of * 8 + i_of, sign, 0.0
    )
    order = order.astype(BF16)

    perm_row = lax.broadcasted_iota(jnp.int32, (ROWS, ROWS), 0)
    perm_col = lax.broadcasted_iota(jnp.int32, (ROWS, ROWS), 1)
    perm_from = perm_row % 16 // 2 * HALF + perm_row // 16 * 2 + perm_row % 2
    perm = jnp.where(perm_col == perm_from, 1.0, 0.0).astype(BF16)

    for step in ORDER:
        came = (z + DEEP - step) % DEEP
        pltpu.make_async_remote_copy(
            src_ref=abuf.at[kb],
            dst_ref=abuf.at[kb],
            send_sem=h1_send,
            recv_sem=h1_recv.at[came],
            device_id=sibling,
            device_id_type=MESH,
        ).wait_recv()
        forward(came * 2 + core)
    forwarded = pltpu.make_async_remote_copy(
        src_ref=abuf.at[pl.ds(0, DEEP)],
        dst_ref=abuf.at[pl.ds(0, DEEP)],
        send_sem=fwd_send,
        recv_sem=fwd_recv,
        device_id=sibling,
        device_id_type=MESH,
    )
    forwarded.wait_recv()
    pl.semaphore_wait(ready, 3)
    for p in range(KC):
        label = beta[p]
        both = jnp.concatenate([abuf[label], abuf[partner[label]]], axis=0)
        sym = jnp.dot(order, both, preferred_element_type=F32).astype(BF16)
        symbuf[0, p] = sym[:HALF]
        symbuf[1, p] = sym[HALF:]
    def send_rows(h):
        lhs[h, pos] = symbuf[h, kc]

        @pl.loop(1, POS)
        def _(step):
            to = (pos + step) % POS
            pltpu.make_async_remote_copy(
                src_ref=symbuf.at[h, to // OCC],
                dst_ref=lhs.at[h, pos],
                send_sem=h2_send.at[h],
                recv_sem=h2_recv.at[h],
                device_id=place(to, kb),
                device_id_type=MESH,
            ).start()

    def lhs_wait(h):
        return pltpu.make_async_remote_copy(
            src_ref=lhs.at[h, pl.ds(0, POS - 1)],
            dst_ref=lhs.at[h, pl.ds(0, POS - 1)],
            send_sem=h2_send.at[h],
            recv_sem=h2_recv.at[h],
            device_id=sibling,
            device_id_type=MESH,
        )

    def multiply(unit, h, first, last):
        acc[unit][...] = jnp.zeros_like(acc[unit])
        left = jnp.concatenate(
            [
                lhs[h, 0:GROUPS].reshape(ROWS, LANES),
                lhs[h, GROUPS:POS].reshape(ROWS, LANES),
            ],
            axis=1,
        )

        @pl.loop(first, last, unroll=2 if unit == 0 else 1)
        def _(step):
            sub = step // (TILES // CHUNK)
            chunk = step % (TILES // CHUNK)
            at = pl.multiple_of(chunk * (CHUNK * 2 * LANES), CHUNK * 2 * LANES)
            down = pl.multiple_of((3 - sub) * DEPTH, DEPTH)
            weight = jnp.concatenate(
                [
                    ztop[pl.ds(down, 4 * DEPTH), pl.ds(at, CHUNK * 2 * LANES)],
                    zbot[pl.ds(down, 4 * DEPTH), pl.ds(at, CHUNK * 2 * LANES)],
                ],
                axis=0,
            )
            product = jnp.dot(left, weight, preferred_element_type=F32)
            den_row = row_den[h, sub]
            parts = []
            for s in range(CHUNK):
                den = den_row + col_den[chunk * CHUNK + s, 0:1, :]
                inverse = jnp.clip(pltpu.reciprocal(den, approx=True), -1.0, 1.0)
                lo = s * 2 * LANES
                parts.append((product[:, lo : lo + LANES] * inverse).astype(BF16))
                parts.append((product[:, lo + LANES : lo + 2 * LANES] * inverse).astype(BF16))
            scaled = jnp.concatenate(parts, axis=1)
            if unit == 0:
                back = weight
            else:
                near = pl.multiple_of((3 - sub % 2) * DEPTH, DEPTH)
                back = jnp.concatenate(
                    [
                        ztop[pl.ds(near, 2 * DEPTH), pl.ds(at, CHUNK * 2 * LANES)],
                        zbot[pl.ds(near, 2 * DEPTH), pl.ds(at, CHUNK * 2 * LANES)],
                    ],
                    axis=0,
                )
            acc[unit][...] += lax.dot_general(
                scaled, back, (((1,), (1,)), ((), ())), preferred_element_type=F32
            )

    def send_partials(unit):
        sums = acc[unit][...].astype(BF16)
        packed = jnp.dot(perm, sums, preferred_element_type=F32).astype(BF16)
        for r in range(POS):
            o1_send[unit][r] = packed[r * 16 : (r + 1) * 16]
        o1_recv[unit][pos] = o1_send[unit][pos]

        @pl.loop(1, POS)
        def _(step):
            to = (pos + step) % POS
            pltpu.make_async_remote_copy(
                src_ref=o1_send[unit].at[to],
                dst_ref=o1_recv[unit].at[pos],
                send_sem=p1_send.at[unit],
                recv_sem=p1_recv.at[unit],
                device_id=place(to, kb),
                device_id_type=MESH,
            ).start()

    def partials_wait(unit):
        return pltpu.make_async_remote_copy(
            src_ref=o1_send[unit].at[pl.ds(0, POS - 1)],
            dst_ref=o1_recv[unit].at[pl.ds(0, POS - 1)],
            send_sem=p1_send.at[unit],
            recv_sem=p1_recv.at[unit],
            device_id=sibling,
            device_id_type=MESH,
        )

    def send_sums(unit):
        partials_wait(unit).wait_recv()
        for label in range(KB):
            at = holder[label] * OCC
            total = o1_recv[unit][at].astype(F32) + o1_recv[unit][at + 1].astype(F32)
            o2_send[unit][label] = total.astype(BF16)
        o2_recv[unit][kb] = o2_send[unit][kb]

        @pl.loop(1, KB)
        def _(step):
            to = (kb + step) % KB
            pltpu.make_async_remote_copy(
                src_ref=o2_send[unit].at[to],
                dst_ref=o2_recv[unit].at[kb],
                send_sem=p2_send.at[unit],
                recv_sem=p2_recv.at[unit],
                device_id={"kb": to},
                device_id_type=MESH,
            ).start()

    def sums_wait(unit):
        return pltpu.make_async_remote_copy(
            src_ref=o2_send[unit].at[pl.ds(0, KB - 1)],
            dst_ref=o2_recv[unit].at[pl.ds(0, KB - 1)],
            send_sem=p2_send.at[unit],
            recv_sem=p2_recv.at[unit],
            device_id=sibling,
            device_id_type=MESH,
        )

    def total_of(unit):
        sums_wait(unit).wait_recv()
        total = o2_recv[unit][0].astype(F32)
        for label in range(1, KB):
            total = total + o2_recv[unit][label].astype(F32)
        return total

    def finish(h, parts):
        for c in range(2):
            for g in range(GROUPS):
                out[0, c, 2 * h : 2 * h + 2, g * LANES : (g + 1) * LANES] = parts[c][
                    2 * g : 2 * g + 2
                ]

    steps = 4 * TILES // CHUNK
    half = steps // 2
    send_rows(0)
    lhs_wait(0).wait_recv()
    send_rows(1)
    multiply(0, 0, 0, steps)
    send_partials(0)
    lhs_wait(1).wait_recv()
    multiply(1, 1, 0, half)
    send_partials(1)
    send_sums(0)
    multiply(2, 1, half, steps)
    send_partials(2)
    send_sums(1)
    send_sums(2)
    whole = total_of(0)
    finish(0, (whole[:, :LANES], whole[:, LANES:]))
    pltpu.make_async_remote_copy(
        src_ref=abuf.at[pl.ds(0, DEEP - 1)],
        dst_ref=abuf.at[pl.ds(0, DEEP - 1)],
        send_sem=h1_send,
        recv_sem=fwd_recv,
        device_id=sibling,
        device_id_type=MESH,
    ).wait_send()
    forwarded.wait_send()
    for h in range(2):
        lhs_wait(h).wait_send()
    for unit in range(3):
        partials_wait(unit).wait_send()
    lane = lax.broadcasted_iota(jnp.int32, (16, LANES), 1)
    first = total_of(1)
    second = total_of(2)
    finish(
        1,
        (
            jnp.where(lane < 64, first, pltpu.roll(second, 64, 1)),
            jnp.where(lane < 64, pltpu.roll(first, 64, 1), second),
        ),
    )
    for unit in range(3):
        sums_wait(unit).wait_send()


def shards(amplitudes, integrals, eps_occ, eps_vir, conserve, partner):
    return pl.pallas_call(
        kernel,
        out_shape=jax.ShapeDtypeStruct((1, 2, 4, GROUPS * LANES), F32),
        in_specs=[pl.BlockSpec(memory_space=pl.ANY)] * 6,
        out_specs=pl.BlockSpec(memory_space=pltpu.VMEM),
        scratch_shapes=[
            pltpu.SMEM((KB, KB), jnp.int32),
            pltpu.SMEM((KB,), jnp.int32),
            pltpu.SMEM((8,), F32),
            pltpu.SMEM((KB, DEPTH), F32),
            pltpu.VMEM((1, 2, DEPTH, 4, 1024), BF16),
            pltpu.SemaphoreType.DMA((5,)),
            pltpu.VMEM((KB, PAIRS, LANES), BF16),
            pltpu.VMEM((2, KC, HALF, LANES), BF16),
            pltpu.VMEM((2, POS, HALF, LANES), BF16),
            pltpu.VMEM((7 * DEPTH, TILES * 2 * LANES), BF16),
            pltpu.VMEM((7 * DEPTH, TILES * 2 * LANES), BF16),
            pltpu.VMEM((2, 4, ROWS, LANES), F32),
            pltpu.VMEM((TILES, 8, LANES), F32),
            pltpu.VMEM((ROWS, 2 * LANES), F32),
            pltpu.VMEM((ROWS, LANES), F32),
        ]
        + [pltpu.VMEM((POS, 16, width), BF16) for width in WIDTHS]
        + [pltpu.VMEM((POS + OCC, 16, width), BF16) for width in WIDTHS]
        + [pltpu.VMEM((KB, 16, width), BF16) for width in WIDTHS] * 2
        + [
            pltpu.SMEM((KC,), jnp.int32),
            pltpu.SMEM((KB,), jnp.int32),
            pltpu.SemaphoreType.REGULAR,
            pltpu.SemaphoreType.DMA,
            pltpu.SemaphoreType.DMA,
            pltpu.SemaphoreType.DMA((DEEP,)),
            pltpu.SemaphoreType.DMA,
            pltpu.SemaphoreType.DMA,
        ]
        + [pltpu.SemaphoreType.DMA((2,))] * 2
        + [pltpu.SemaphoreType.DMA((3,))] * 4,
        compiler_params=pltpu.CompilerParams(
            collective_id=0, has_side_effects=True, vmem_limit_bytes=60 * 2**20
        ),
        name="lambda_source",
    )(conserve, partner, eps_occ, eps_vir, amplitudes, integrals)


def solution(mesh):
    in_specs = (P("kb", None, None, None), P("kb", None, None, "occ", None), P(), P(), P(), P())
    out_specs = P("kb", None, ("kc", "occ"), None)
    return jax.shard_map(shards, mesh=mesh, in_specs=in_specs, out_specs=out_specs, check_vma=False)
```

```python
import functools

import jax
import jax.numpy as jnp
from jax import lax
from jax.experimental import pallas as pl
from jax.experimental.pallas import tpu as pltpu
from jax.sharding import PartitionSpec as P

KC = 8
KB = 16
OCC = 2
POS = KC * OCC
LANES = 128
PAIRS = 64
GROUPS = 8
HALF = 32
ROWS = GROUPS * HALF
DEPTH = 32
TILES = 32
CHUNK = 32
SHIFT = 2.0**-18
WIDTHS = (2 * LANES, LANES, LANES)
DEEP = 8
ORDER = (1, 7, 2, 6, 3, 5, 4)
MESH = pl.DeviceIdType.MESH
F32 = jnp.float32
BF16 = jnp.bfloat16


def place(position, kb):
    return {"kc": position // OCC, "kb": kb, "occ": position % OCC}


def kernel(
    conserve_in, partner_in, eps_occ_in, eps_vir_in, amp, slab_in, out,
    conserve, partner, eps_occ, eps_vir, slab, load_sem, abuf, symbuf, lhs, ztop, zbot, row_den, col_den, acc0, acc1,
    o1_send0, o1_send1, o1_send2, o1_recv0, o1_recv1, o1_recv2,
    o2_send0, o2_send1, o2_send2, o2_recv0, o2_recv1, o2_recv2, beta, holder, ready, copy_sem,
    h1_send, h1_recv, fwd_send, fwd_recv, h2_send, h2_recv, p1_send, p1_recv, p2_send, p2_recv,
):
    kc = lax.axis_index("kc")
    kb = lax.axis_index("kb")
    occ = lax.axis_index("occ")
    pos = kc * OCC + occ
    core = kb % 2
    z = kb // 2
    sibling = {"kb": kb + 1 - 2 * core}
    part = pos // GROUPS
    group = pos % GROUPS
    x = kc // 2
    y_lo = kc % 2
    y = occ * 2 + y_lo

    def along_z(step):
        return {"kb": (z + step) % DEEP * 2 + core}

    def along_y(step):
        to = (y + step) % 4
        return {"kc": x * 2 + to % 2, "occ": to // 2}

    acc = (acc0, acc1, acc1)
    o1_send = (o1_send0, o1_send1, o1_send2)
    o1_recv = (o1_recv0, o1_recv1, o1_recv2)
    o2_send = (o2_send0, o2_send1, o2_send2)
    o2_recv = (o2_recv0, o2_recv1, o2_recv2)
    barrier = pltpu.get_barrier_semaphore()

    own = pltpu.make_async_copy(
        amp.at[0, part, :, pl.ds(pl.multiple_of(group * LANES, LANES), LANES)],
        abuf.at[kb],
        copy_sem,
    )
    own.start()
    for step in ORDER:
        pl.semaphore_signal(barrier, inc=1, device_id=along_z(step), device_id_type=MESH)
    pl.semaphore_signal(barrier, inc=1, device_id=sibling, device_id_type=MESH)
    for step in range(1, 4):
        pl.semaphore_signal(
            barrier,
            inc=1,
            device_id={"kc": (x + step) % 4 * 2 + y_lo},
            device_id_type=MESH,
        )
        pl.semaphore_signal(barrier, inc=1, device_id=along_y(step), device_id_type=MESH)

    loads = [
        pltpu.make_async_copy(source, target, load_sem.at[at])
        for at, (source, target) in enumerate(
            (
                (slab_in, slab),
                (conserve_in, conserve),
                (partner_in, partner),
                (eps_occ_in, eps_occ),
                (eps_vir_in, eps_vir),
            )
        )
    ]
    for load in loads:
        load.start()
    own.wait()
    pl.semaphore_wait(barrier, DEEP + 6)

    def stripe_copy(step):
        return pltpu.make_async_remote_copy(
            src_ref=abuf.at[kb],
            dst_ref=abuf.at[kb],
            send_sem=h1_send,
            recv_sem=h1_recv.at[z],
            device_id=along_z(step),
            device_id_type=MESH,
        )

    def forward(label):
        pltpu.make_async_remote_copy(
            src_ref=abuf.at[label],
            dst_ref=abuf.at[label],
            send_sem=fwd_send,
            recv_sem=fwd_recv,
            device_id=sibling,
            device_id_type=MESH,
        ).start()

    for step in ORDER:
        stripe_copy(step).start()
    for step in range(1, 4):
        pl.semaphore_signal(ready, inc=1, device_id=along_y(step), device_id_type=MESH)
    forward(kb)

    ztop[...] = jnp.zeros_like(ztop)
    zbot[...] = jnp.zeros_like(zbot)
    for load in loads:
        load.wait()
    for k in range(4):
        real = slab[0, 0, :, k, :]
        imag = slab[0, 1, :, k, :]
        for u in range(8):
            at = (k * 8 + u) * 2 * LANES
            re = real[:, u * LANES : (u + 1) * LANES]
            im = imag[:, u * LANES : (u + 1) * LANES]
            ztop[3 * DEPTH : 4 * DEPTH, at : at + LANES] = re
            ztop[3 * DEPTH : 4 * DEPTH, at + LANES : at + 2 * LANES] = im
            zbot[3 * DEPTH : 4 * DEPTH, at : at + LANES] = -im
            zbot[3 * DEPTH : 4 * DEPTH, at + LANES : at + 2 * LANES] = re

    for p in range(KC):
        found = jnp.int32(0)
        for label in range(KB):
            found = found + jnp.where(conserve[label, p] == kb, label, 0)
        beta[p] = jnp.minimum(found, KB - 1)
    for label in range(KB):
        left = jnp.int32(KC)
        for p in range(KC):
            left = left - jnp.where(conserve[label, p] == kb, KC - p, 0)
        holder[label] = jnp.maximum(left, 0)
    mine = jnp.int32(0)
    for label in range(KB):
        mine = mine + jnp.where(conserve[label, kc] == kb, label, 0)
    mine = jnp.minimum(mine, KB - 1)

    row = lax.broadcasted_iota(jnp.int32, (HALF, LANES), 0)
    lane = lax.broadcasted_iota(jnp.int32, (8, LANES), 1)
    for h in range(2):
        i_of = row // 4
        j_of = (row // 2) % 2 * 4 + h * 2 + row % 2
        pair = jnp.full((HALF, LANES), -SHIFT, F32)
        for k in range(8):
            pair = pair + jnp.where(i_of == k, eps_occ[k], 0.0)
            pair = pair + jnp.where(j_of == k, eps_occ[k], 0.0)
        for a in range(DEPTH):
            g, sub = a // 4, a % 4
            row_den[h, sub, g * HALF : (g + 1) * HALF, :] = pair - eps_vir[mine, a]
    vir_c = jnp.zeros((8, LANES), F32)
    for c in range(DEPTH):
        vir_c = vir_c + jnp.where(lane % DEPTH == c, eps_vir[kb, c], 0.0)
    for u in range(8):
        vir_bc = vir_c
        for s in range(4):
            vir_bc = vir_bc + jnp.where(lane // DEPTH == s, eps_vir[kc, u * 4 + s], 0.0)
        for k in range(4):
            col_den[k * 8 + u] = eps_occ[occ * 4 + k] - vir_bc

    for landing in o1_recv:
        for zero in range(OCC):
            landing[POS + zero] = jnp.zeros(landing.shape[1:], BF16)

    out_row = lax.broadcasted_iota(jnp.int32, (PAIRS, 2 * PAIRS), 0)
    in_col = lax.broadcasted_iota(jnp.int32, (PAIRS, 2 * PAIRS), 1)
    h_of = out_row // HALF
    i_of = out_row % HALF // 4
    j_of = out_row % HALF // 2 % 2 * 4 + h_of * 2 + out_row % 2
    sign = (1 - 2 * part).astype(F32)
    order = jnp.where(in_col == i_of * 8 + j_of, 1.0, 0.0) + jnp.where(
        in_col == PAIRS + j_of * 8 + i_of, sign, 0.0
    )
    order = order.astype(BF16)

    perm_row = lax.broadcasted_iota(jnp.int32, (ROWS, ROWS), 0)
    perm_col = lax.broadcasted_iota(jnp.int32, (ROWS, ROWS), 1)
    perm_from = perm_row % 16 // 2 * HALF + perm_row // 16 * 2 + perm_row % 2
    perm = jnp.where(perm_col == perm_from, 1.0, 0.0).astype(BF16)

    for step in ORDER:
        came = (z + DEEP - step) % DEEP
        pltpu.make_async_remote_copy(
            src_ref=abuf.at[kb],
            dst_ref=abuf.at[kb],
            send_sem=h1_send,
            recv_sem=h1_recv.at[came],
            device_id=sibling,
            device_id_type=MESH,
        ).wait_recv()
        forward(came * 2 + core)
    forwarded = pltpu.make_async_remote_copy(
        src_ref=abuf.at[pl.ds(0, DEEP)],
        dst_ref=abuf.at[pl.ds(0, DEEP)],
        send_sem=fwd_send,
        recv_sem=fwd_recv,
        device_id=sibling,
        device_id_type=MESH,
    )
    forwarded.wait_recv()
    pl.semaphore_wait(ready, 3)
    for p in range(KC):
        label = beta[p]
        both = jnp.concatenate([abuf[label], abuf[partner[label]]], axis=0)
        sym = jnp.dot(order, both, preferred_element_type=F32).astype(BF16)
        symbuf[0, p] = sym[:HALF]
        symbuf[1, p] = sym[HALF:]
    def send_rows(h):
        lhs[h, pos] = symbuf[h, kc]

        @pl.loop(1, POS)
        def _(step):
            to = (pos + step) % POS
            pltpu.make_async_remote_copy(
                src_ref=symbuf.at[h, to // OCC],
                dst_ref=lhs.at[h, pos],
                send_sem=h2_send.at[h],
                recv_sem=h2_recv.at[h],
                device_id=place(to, kb),
                device_id_type=MESH,
            ).start()

    def lhs_wait(h):
        return pltpu.make_async_remote_copy(
            src_ref=lhs.at[h, pl.ds(0, POS - 1)],
            dst_ref=lhs.at[h, pl.ds(0, POS - 1)],
            send_sem=h2_send.at[h],
            recv_sem=h2_recv.at[h],
            device_id=sibling,
            device_id_type=MESH,
        )

    def multiply(unit, h, first, last):
        acc[unit][...] = jnp.zeros_like(acc[unit])
        left = jnp.concatenate(
            [
                lhs[h, 0:GROUPS].reshape(ROWS, LANES),
                lhs[h, GROUPS:POS].reshape(ROWS, LANES),
            ],
            axis=1,
        )

        @pl.loop(first, last, unroll=2 if unit < 2 else 1)
        def _(step):
            sub = step // (TILES // CHUNK)
            chunk = step % (TILES // CHUNK)
            at = pl.multiple_of(chunk * (CHUNK * 2 * LANES), CHUNK * 2 * LANES)
            down = pl.multiple_of((3 - sub) * DEPTH, DEPTH)
            weight = jnp.concatenate(
                [
                    ztop[pl.ds(down, 4 * DEPTH), pl.ds(at, CHUNK * 2 * LANES)],
                    zbot[pl.ds(down, 4 * DEPTH), pl.ds(at, CHUNK * 2 * LANES)],
                ],
                axis=0,
            )
            product = jnp.dot(left, weight, preferred_element_type=F32)
            den_row = row_den[h, sub]
            parts = []
            for s in range(CHUNK):
                den = den_row + col_den[chunk * CHUNK + s, 0:1, :]
                inverse = jnp.clip(pltpu.reciprocal(den, approx=True), -1.0, 1.0)
                lo = s * 2 * LANES
                parts.append((product[:, lo : lo + LANES] * inverse).astype(BF16))
                parts.append((product[:, lo + LANES : lo + 2 * LANES] * inverse).astype(BF16))
            scaled = jnp.concatenate(parts, axis=1)
            if unit == 0:
                back = weight
            else:
                near = pl.multiple_of((3 - sub % 2) * DEPTH, DEPTH)
                back = jnp.concatenate(
                    [
                        ztop[pl.ds(near, 2 * DEPTH), pl.ds(at, CHUNK * 2 * LANES)],
                        zbot[pl.ds(near, 2 * DEPTH), pl.ds(at, CHUNK * 2 * LANES)],
                    ],
                    axis=0,
                )
            acc[unit][...] += lax.dot_general(
                scaled, back, (((1,), (1,)), ((), ())), preferred_element_type=F32
            )

    def send_partials(unit):
        sums = acc[unit][...].astype(BF16)
        packed = jnp.dot(perm, sums, preferred_element_type=F32).astype(BF16)
        for r in range(POS):
            o1_send[unit][r] = packed[r * 16 : (r + 1) * 16]
        o1_recv[unit][pos] = o1_send[unit][pos]

        @pl.loop(1, POS)
        def _(step):
            to = (pos + step) % POS
            pltpu.make_async_remote_copy(
                src_ref=o1_send[unit].at[to],
                dst_ref=o1_recv[unit].at[pos],
                send_sem=p1_send.at[unit],
                recv_sem=p1_recv.at[unit],
                device_id=place(to, kb),
                device_id_type=MESH,
            ).start()

    def partials_wait(unit):
        return pltpu.make_async_remote_copy(
            src_ref=o1_send[unit].at[pl.ds(0, POS - 1)],
            dst_ref=o1_recv[unit].at[pl.ds(0, POS - 1)],
            send_sem=p1_send.at[unit],
            recv_sem=p1_recv.at[unit],
            device_id=sibling,
            device_id_type=MESH,
        )

    def send_sums(unit):
        partials_wait(unit).wait_recv()
        for label in range(KB):
            at = holder[label] * OCC
            total = o1_recv[unit][at].astype(F32) + o1_recv[unit][at + 1].astype(F32)
            o2_send[unit][label] = total.astype(BF16)
        o2_recv[unit][kb] = o2_send[unit][kb]

        @pl.loop(1, KB)
        def _(step):
            to = (kb + step) % KB
            pltpu.make_async_remote_copy(
                src_ref=o2_send[unit].at[to],
                dst_ref=o2_recv[unit].at[kb],
                send_sem=p2_send.at[unit],
                recv_sem=p2_recv.at[unit],
                device_id={"kb": to},
                device_id_type=MESH,
            ).start()

    def sums_wait(unit):
        return pltpu.make_async_remote_copy(
            src_ref=o2_send[unit].at[pl.ds(0, KB - 1)],
            dst_ref=o2_recv[unit].at[pl.ds(0, KB - 1)],
            send_sem=p2_send.at[unit],
            recv_sem=p2_recv.at[unit],
            device_id=sibling,
            device_id_type=MESH,
        )

    def total_of(unit):
        sums_wait(unit).wait_recv()
        total = o2_recv[unit][0].astype(F32)
        for label in range(1, KB):
            total = total + o2_recv[unit][label].astype(F32)
        return total

    def finish(h, parts):
        for c in range(2):
            for g in range(GROUPS):
                out[0, c, 2 * h : 2 * h + 2, g * LANES : (g + 1) * LANES] = parts[c][
                    2 * g : 2 * g + 2
                ]

    steps = 4 * TILES // CHUNK
    half = steps // 2
    send_rows(0)
    lhs_wait(0).wait_recv()
    send_rows(1)
    multiply(0, 0, 0, steps)
    send_partials(0)
    lhs_wait(1).wait_recv()
    multiply(1, 1, 0, half)
    send_partials(1)
    send_sums(0)
    multiply(2, 1, half, steps)
    send_partials(2)
    send_sums(1)
    whole = total_of(0)
    finish(0, (whole[:, :LANES], whole[:, LANES:]))
    send_sums(2)
    pltpu.make_async_remote_copy(
        src_ref=abuf.at[pl.ds(0, DEEP - 1)],
        dst_ref=abuf.at[pl.ds(0, DEEP - 1)],
        send_sem=h1_send,
        recv_sem=fwd_recv,
        device_id=sibling,
        device_id_type=MESH,
    ).wait_send()
    forwarded.wait_send()
    for h in range(2):
        lhs_wait(h).wait_send()
    for unit in range(3):
        partials_wait(unit).wait_send()
    lane = lax.broadcasted_iota(jnp.int32, (16, LANES), 1)
    first = total_of(1)
    second = total_of(2)
    finish(
        1,
        (
            jnp.where(lane < 64, first, pltpu.roll(second, 64, 1)),
            jnp.where(lane < 64, pltpu.roll(first, 64, 1), second),
        ),
    )
    for unit in range(3):
        sums_wait(unit).wait_send()


def shards(amplitudes, integrals, eps_occ, eps_vir, conserve, partner):
    return pl.pallas_call(
        kernel,
        out_shape=jax.ShapeDtypeStruct((1, 2, 4, GROUPS * LANES), F32),
        in_specs=[pl.BlockSpec(memory_space=pl.ANY)] * 6,
        out_specs=pl.BlockSpec(memory_space=pltpu.VMEM),
        scratch_shapes=[
            pltpu.SMEM((KB, KB), jnp.int32),
            pltpu.SMEM((KB,), jnp.int32),
            pltpu.SMEM((8,), F32),
            pltpu.SMEM((KB, DEPTH), F32),
            pltpu.VMEM((1, 2, DEPTH, 4, 1024), BF16),
            pltpu.SemaphoreType.DMA((5,)),
            pltpu.VMEM((KB, PAIRS, LANES), BF16),
            pltpu.VMEM((2, KC, HALF, LANES), BF16),
            pltpu.VMEM((2, POS, HALF, LANES), BF16),
            pltpu.VMEM((7 * DEPTH, TILES * 2 * LANES), BF16),
            pltpu.VMEM((7 * DEPTH, TILES * 2 * LANES), BF16),
            pltpu.VMEM((2, 4, ROWS, LANES), F32),
            pltpu.VMEM((TILES, 8, LANES), F32),
            pltpu.VMEM((ROWS, 2 * LANES), F32),
            pltpu.VMEM((ROWS, LANES), F32),
        ]
        + [pltpu.VMEM((POS, 16, width), BF16) for width in WIDTHS]
        + [pltpu.VMEM((POS + OCC, 16, width), BF16) for width in WIDTHS]
        + [pltpu.VMEM((KB, 16, width), BF16) for width in WIDTHS] * 2
        + [
            pltpu.SMEM((KC,), jnp.int32),
            pltpu.SMEM((KB,), jnp.int32),
            pltpu.SemaphoreType.REGULAR,
            pltpu.SemaphoreType.DMA,
            pltpu.SemaphoreType.DMA,
            pltpu.SemaphoreType.DMA((DEEP,)),
            pltpu.SemaphoreType.DMA,
            pltpu.SemaphoreType.DMA,
        ]
        + [pltpu.SemaphoreType.DMA((2,))] * 2
        + [pltpu.SemaphoreType.DMA((3,))] * 4,
        compiler_params=pltpu.CompilerParams(
            collective_id=0, has_side_effects=True, vmem_limit_bytes=60 * 2**20
        ),
        name="lambda_source",
    )(conserve, partner, eps_occ, eps_vir, amplitudes, integrals)


def solution(mesh):
    in_specs = (P("kb", None, None, None), P("kb", None, None, "occ", None), P(), P(), P(), P())
    out_specs = P("kb", None, ("kc", "occ"), None)
    return jax.shard_map(shards, mesh=mesh, in_specs=in_specs, out_specs=out_specs, check_vma=False)
```
